256 devices in a mesh: dp: 32 (over z, x_hi, core), tensor: 8 (over x_lo, y).
Axes of the slice: x: 4 (x_hi: 2, x_lo: 2; x = x_hi * 2 + x_lo), y: 4, z: 8, core: 2. Of those that a mesh axis runs over, the one named last changes fastest.
Arguments:
- tokens: bfloat16 [8192, 8192], P('dp', 'tensor'), may hold values from -6 to 6
- out_grad: bfloat16 [8192, 8, 256], P('dp', 'tensor'), may hold values from -2 to 2
- active: int32 [32, 8, 2], P('dp', 'tensor'), may hold values from 0 to 28, as said below
- w_gate: bfloat16 [8192, 28672], P('dp', 'tensor'), may hold values from -0.0625 to 0.0625
- w_up: bfloat16 [8192, 28672], P('dp', 'tensor'), may hold values from -0.0625 to 0.0625
Outputs:
- input_grad: bfloat16 [8192, 8192], P('dp', 'tensor')
- gate_weight_grad: bfloat16 [8192, 28672], P('dp', 'tensor')
- up_weight_grad: bfloat16 [8192, 28672], P('dp', 'tensor')
The draws below stay inside these ranges and needn't reach their ends.
Inputs may be any that keep to these rules, and one draw needn't show every extreme that they name: `active`: each entry is a block number of the shard or 28 for an empty slot. In every tile and shard the live entries come first, are distinct and number at least one; in every tile some shard has all 2 slots live.
All inputs are finite; a program needn't handle non-finite values.
Results may differ from the reference program's by a relative error of at most 0.014.
Values may be sent and summed in bfloat16 or wider, within the bound.
A program may use at most 128 MiB of HBM per device.

```python
import jax
import jax.numpy as jnp
from jax import lax

D = 8192
FF = 28672
BLOCK = 128
TILE = 256
CAP = 2
SHARDS = 8
BPS = 28
TILES = 32
TOKENS = 8192


def draw_active(key, part):
    key_scores, key_counts, key_full = jax.random.split(key, 3)
    scores = jax.random.randint(key_scores, (TILES, SHARDS, BPS), 0, 1 << 20) * BPS + jnp.arange(BPS, dtype=jnp.int32)
    chosen = jnp.sort(jnp.argsort(scores, axis=-1)[..., :CAP], axis=-1).astype(jnp.int32)
    counts = jax.random.randint(key_counts, (TILES, SHARDS), 1, CAP + 1)
    full_shard = jax.random.randint(key_full, (TILES,), 0, SHARDS)
    counts = jnp.where(jnp.arange(SHARDS)[None, :] == full_shard[:, None], CAP, counts)
    slot_index = jnp.arange(CAP)[None, None, :]
    return jnp.where(slot_index < counts[..., None], chosen, BPS).astype(jnp.int32)


def levels(rng, extent, shards, least, largest):
    gain, own = 1.0, jax.random.fold_in(rng, 6)
    for axis_at, blocks in shards:
        heights = jnp.exp(jax.random.uniform(jax.random.fold_in(own, axis_at), (blocks,), jnp.float32, least / len(shards), largest / len(shards)))
        gain = gain * jnp.repeat(heights, extent[axis_at] // blocks).reshape([-1 if axis == axis_at else 1 for axis in range(len(extent))])
    return gain


def scatter_about(stream_key, extent, deviation, bound, pieces=(), held_as=jnp.bfloat16):
    values = jax.random.normal(stream_key, extent, jnp.float32) * deviation
    if len(pieces) > 0:
        values = levels(stream_key, extent, pieces, -0.22, 0.18) * values
    return jnp.clip(values, min=-bound, max=bound).astype(held_as)


def setup_inputs(seed: int = 0) -> dict:
    keys = jax.random.split(jax.random.key(seed), 6)
    return {
        "tokens": scatter_about(keys[0], (TOKENS, D), 1.0, 6.0, ((0, 32), (1, 8))),
        "out_grad": scatter_about(keys[1], (TOKENS, SHARDS, CAP * BLOCK), 0.3, 2.0, ((0, 32), (1, 8))),
        "active": draw_active(jax.random.fold_in(keys[5], 71), 0),
        "w_gate": scatter_about(keys[3], (D, FF), D ** -0.5, 0.0625, ((0, 32), (1, 8))),
        "w_up": scatter_about(keys[4], (D, FF), D ** -0.5, 0.0625, ((0, 32), (1, 8))),
    }


def reference(tokens, out_grad, active, w_gate, w_up):
    gate_shaped = w_gate.reshape(D, SHARDS, BPS, BLOCK)
    up_shaped = w_up.reshape(D, SHARDS, BPS, BLOCK)
    shard_ids = jnp.arange(SHARDS).astype(jnp.int32)[:, None]
    unit_ids = jnp.arange(BLOCK).astype(jnp.int32)

    def one_tile(carry, inputs):
        gate_total, up_total = carry
        tile_rows, tile_grad, tile_active = inputs
        alive = (tile_active < BPS).astype(jnp.float32)
        picked = jnp.minimum(tile_active, BPS - 1).astype(jnp.int32)
        gate_cols = gate_shaped[:, shard_ids, picked]
        up_cols = up_shaped[:, shard_ids, picked]
        gate_flat = gate_cols.reshape(D, SHARDS * CAP * BLOCK)
        up_flat = up_cols.reshape(D, SHARDS * CAP * BLOCK)
        gate_value = jnp.dot(tile_rows, gate_flat, preferred_element_type=jnp.float32).reshape(TILE, SHARDS, CAP, BLOCK)
        up_value = jnp.dot(tile_rows, up_flat, preferred_element_type=jnp.float32).reshape(TILE, SHARDS, CAP, BLOCK)
        upstream = tile_grad.astype(jnp.float32).reshape(TILE, SHARDS, CAP, BLOCK)
        alive_mask = alive[None, :, :, None]
        positive = jnp.maximum(gate_value, 0.0)
        gate_grad = (upstream * up_value * 2.0 * positive * alive_mask).astype(jnp.bfloat16)
        up_grad = (upstream * positive * positive * alive_mask).astype(jnp.bfloat16)
        partial_value = jnp.einsum("nsck,dsck->nsd", gate_grad.astype(jnp.float32), gate_cols.astype(jnp.float32))
        partial_value = partial_value + jnp.einsum("nsck,dsck->nsd", up_grad.astype(jnp.float32), up_cols.astype(jnp.float32))
        rounded = lax.optimization_barrier(partial_value.astype(jnp.bfloat16)).astype(jnp.float32)
        input_tile = jnp.sum(rounded, axis=1).astype(jnp.bfloat16)
        gate_piece = jnp.dot(tile_rows.T, gate_grad.reshape(TILE, SHARDS * CAP * BLOCK), preferred_element_type=jnp.float32)
        up_piece = jnp.dot(tile_rows.T, up_grad.reshape(TILE, SHARDS * CAP * BLOCK), preferred_element_type=jnp.float32)
        gate_piece = lax.optimization_barrier(gate_piece.astype(jnp.bfloat16)).astype(jnp.float32)
        up_piece = lax.optimization_barrier(up_piece.astype(jnp.bfloat16)).astype(jnp.float32)
        columns = ((shard_ids * BPS + picked)[:, :, None] * BLOCK + unit_ids[None, None, :]).reshape(-1).astype(jnp.int32)
        gate_total = gate_total.at[:, columns].add(gate_piece)
        up_total = up_total.at[:, columns].add(up_piece)
        return (gate_total, up_total), input_tile

    start = (jnp.zeros((D, FF), jnp.float32), jnp.zeros((D, FF), jnp.float32))
    inputs = (tokens.reshape(TILES, TILE, D), out_grad.reshape(TILES, TILE, SHARDS, CAP * BLOCK), active)
    (gate_total, up_total), input_tiles = lax.scan(one_tile, start, inputs)
    input_grad = input_tiles.reshape(TOKENS, D)
    return input_grad, gate_total.astype(jnp.bfloat16), up_total.astype(jnp.bfloat16)
```

```python
import jax
import jax.numpy as jnp
from jax import lax
from jax.experimental import pallas as pl
from jax.experimental.pallas import tpu as pltpu
from jax.sharding import PartitionSpec as P

BLOCK = 128
TILE = 256
CAP = 2


def block_columns(w_ref, block):
    return w_ref[:, pl.ds(pl.multiple_of(block * BLOCK, BLOCK), BLOCK)]


def listed_weights(listed, tile, blocks, gate_ref, up_ref):
    picked = [jnp.minimum(listed[tile * CAP + c], blocks - 1) for c in range(CAP)]
    columns = [block_columns(ref, b) for ref in (gate_ref, up_ref) for b in picked]
    return picked, jnp.concatenate(columns, axis=1)


def forward_kernel(listed, tok_ref, gate_ref, up_ref, out_ref):
    blocks = gate_ref.shape[1] // BLOCK
    _, weights = listed_weights(listed, pl.program_id(0), blocks, gate_ref, up_ref)
    rows = gate_ref.shape[0]
    tok = tok_ref[...].reshape(TILE, rows)
    out_ref[0] = jnp.dot(tok, weights, preferred_element_type=jnp.float32).astype(out_ref.dtype)


def backward_kernel(listed, tok_ref, grad_ref, gate_ref, up_ref, part_ref, dgate_ref, dup_ref, gate_acc, up_acc):
    blocks = gate_ref.shape[1] // BLOCK
    tile = pl.program_id(0)
    rows = gate_ref.shape[0]

    @pl.when(tile == 0)
    def _():
        gate_acc[...] = jnp.zeros_like(gate_acc)
        up_acc[...] = jnp.zeros_like(up_acc)

    picked, weights = listed_weights(listed, tile, blocks, gate_ref, up_ref)
    tok = tok_ref[...].reshape(TILE, rows)
    grads = grad_ref[0]
    part = lax.dot_general(grads, weights, (((1,), (1,)), ((), ())), preferred_element_type=jnp.float32)
    part_ref[...] = part.astype(part_ref.dtype).reshape(part_ref.shape)
    pieces = lax.dot_general(tok, grads, (((0,), (0,)), ((), ())), preferred_element_type=jnp.float32)
    pieces = pieces.astype(jnp.bfloat16).astype(jnp.float32)
    for k, acc in enumerate((gate_acc, up_acc)):
        for c in range(CAP):
            at = pl.ds(pl.multiple_of(picked[c] * BLOCK, BLOCK), BLOCK)
            acc[:, at] += pieces[:, (k * CAP + c) * BLOCK : (k * CAP + c + 1) * BLOCK]

    @pl.when(tile == pl.num_programs(0) - 1)
    def _():
        dgate_ref[...] = gate_acc[...].astype(dgate_ref.dtype)
        dup_ref[...] = up_acc[...].astype(dup_ref.dtype)


def per_device(tokens, out_grad, active, w_gate, w_up):
    dp, tp = lax.axis_size("dp"), lax.axis_size("tensor")
    rows, width = w_gate.shape
    blocks = width // BLOCK
    share = TILE // tp
    quarter = tokens.shape[1] // rows
    units = 2 * CAP * BLOCK

    listed = lax.all_gather(active.reshape(CAP), "dp", axis=0, tiled=True)

    spread = lax.all_to_all(tokens.reshape(tp, share, -1), "tensor", 0, 0, tiled=True)
    spread = spread.reshape(tp, share, quarter, rows).swapaxes(1, 2).reshape(dp, share, rows)
    mine = lax.all_to_all(spread, "dp", 0, 0, tiled=True)
    toks = lax.all_gather(mine, "tensor", axis=0)

    whole = pl.BlockSpec((rows, width), lambda q, *_: (0, 0))
    tok_spec = pl.BlockSpec((tp, 1, share, rows), lambda q, *_: (0, q, 0, 0))
    tile_spec = pl.BlockSpec((1, TILE, units), lambda q, *_: (q, 0, 0))
    partial = pl.pallas_call(
        forward_kernel,
        grid_spec=pltpu.PrefetchScalarGridSpec(
            num_scalar_prefetch=1, grid=(dp,), in_specs=[tok_spec, whole, whole], out_specs=tile_spec
        ),
        out_shape=jax.ShapeDtypeStruct((dp, TILE, units), jnp.bfloat16),
        compiler_params=pltpu.CompilerParams(vmem_limit_bytes=40 * 2**20),
    )(listed, toks, w_gate, w_up)
    both = lax.psum_scatter(partial, "dp", scatter_dimension=0, tiled=True)[0].astype(jnp.float32)

    gate, up = both[:, : CAP * BLOCK], both[:, CAP * BLOCK :]
    live = (active.reshape(1, CAP, 1) < blocks).astype(jnp.float32)
    live = jnp.broadcast_to(live, (1, CAP, BLOCK)).reshape(1, CAP * BLOCK)
    g = out_grad.reshape(TILE, CAP * BLOCK).astype(jnp.float32)
    relu = jnp.maximum(gate, 0.0)
    gate_grad = (g * up * 2.0 * relu * live).astype(jnp.bfloat16)
    up_grad = (g * relu * relu * live).astype(jnp.bfloat16)
    grads = lax.all_gather(jnp.concatenate([gate_grad, up_grad], axis=1), "dp", axis=0)

    parts, dgate, dup = pl.pallas_call(
        backward_kernel,
        grid_spec=pltpu.PrefetchScalarGridSpec(
            num_scalar_prefetch=1,
            grid=(dp,),
            in_specs=[tok_spec, tile_spec, whole, whole],
            out_specs=[tok_spec, whole, whole],
            scratch_shapes=[pltpu.VMEM((rows, width), jnp.float32)] * 2,
        ),
        out_shape=[
            jax.ShapeDtypeStruct((tp, dp, share, rows), jnp.bfloat16),
            jax.ShapeDtypeStruct((rows, width), jnp.bfloat16),
            jax.ShapeDtypeStruct((rows, width), jnp.bfloat16),
        ],
        compiler_params=pltpu.CompilerParams(vmem_limit_bytes=50 * 2**20),
    )(listed, toks, grads, w_gate, w_up)
    summed = lax.psum_scatter(parts, "tensor", scatter_dimension=0, tiled=True)[0]
    back = lax.all_to_all(summed, "dp", 0, 0, tiled=True)
    back = back.reshape(tp, quarter, share, rows).swapaxes(1, 2).reshape(tp, share, quarter * rows)
    input_grad = lax.all_to_all(back, "tensor", 0, 0, tiled=True).reshape(TILE, quarter * rows)
    return input_grad, dgate, dup


def solution(mesh):
    placed = (
        P("dp", "tensor"),
        P("dp", "tensor", None),
        P("dp", "tensor", None),
        P("dp", "tensor"),
        P("dp", "tensor"),
    )
    return jax.shard_map(
        per_device,
        mesh=mesh,
        in_specs=placed,
        out_specs=(P("dp", "tensor"), P("dp", "tensor"), P("dp", "tensor")),
        check_vma=False,
    )
```

```python
import jax
import jax.numpy as jnp
from jax import lax
from jax.experimental import pallas as pl
from jax.experimental.pallas import tpu as pltpu
from jax.sharding import PartitionSpec as P

MESH = pl.DeviceIdType.MESH
BLOCK, TILE, CAP = 128, 256, 2
NZ, QUARTERS, TENSOR, DP = 8, 4, 8, 32
ROWS = 256
SHARE = TILE // TENSOR
UNITS = 2 * CAP * BLOCK
BF16, F32 = jnp.bfloat16, jnp.float32


def send(src, dst, send_sem, recv_sem, device):
    pltpu.make_async_remote_copy(
        src_ref=src, dst_ref=dst, send_sem=send_sem, recv_sem=recv_sem, device_id=device, device_id_type=MESH
    ).start()


def wait(ref, sem):
    pltpu.make_async_copy(ref, ref, sem).wait()


def main_kernel(
    tokens, live_grad, act, wg_hbm, wu_hbm,
    out, pieces_hbm, listed,
    wg, wu, listed_v, tok, sc, rc, sz, rz, xs, xr, acc, gr, part, piece, yr1, yr2, xr2, fin,
    s_t1, r_t1, s_act, r_act, l_act, s_w, s_x, r_x, s_y, r_y, s_f, r_f, s_c, r_c, s_z, r_z, s_h, r_h,
    s_gh, r_gh, s_gz, r_gz, s_gc, r_gc, s_0, r_0, s_1, r_1, s_2, r_2, s_o, r_o, s_p,
):
    d, t = lax.axis_index("dp"), lax.axis_index("tensor")
    z, a = d // QUARTERS, lax.rem(d, QUARTERS)
    xh, c = a // 2, lax.rem(a, 2)
    xl, y = t // 4, lax.rem(t, 4)
    at_home = t == z

    def plane(dz):
        return lax.rem(z + dz + NZ, NZ)

    up_z, down_z = (plane(1) * 4 + a, t), (plane(-1) * 4 + a, t)
    sibling = (d + 1 - 2 * c, t)
    across = (z * 4 + (1 - xh) * 2 + c, t)
    beside = (d, (1 - xl) * 4 + y)
    y_next, y_last, y_far = lax.rem(y + 1, 4), lax.rem(y + 3, 4), lax.rem(y + 2, 4)
    up_y, down_y = (d, xl * 4 + y_next), (d, xl * 4 + y_last)

    def load_block(b, _):
        columns = pl.ds(pl.multiple_of(b * BLOCK, BLOCK), BLOCK)
        pltpu.make_async_copy(wg_hbm.at[:, columns], wg.at[b], s_w.at[0]).start()
        pltpu.make_async_copy(wu_hbm.at[:, columns], wu.at[b], s_w.at[1]).start()
        return 0

    lax.fori_loop(0, wg.shape[0], load_block, 0)

    barrier = pltpu.get_barrier_semaphore()

    def greet(device):
        pl.semaphore_signal(barrier, inc=1, device_id=device, device_id_type=MESH)

    def spread_to(k):
        return (t * QUARTERS + k // TENSOR, lax.rem(k, TENSOR))

    def greet_all(k, _):
        other = spread_to(k)
        mine = jnp.logical_and(other[0] == d, other[1] == t)

        @pl.when(jnp.logical_not(mine))
        def _():
            greet(other)

        source_is_me = jnp.logical_and(k == d, at_home)

        @pl.when(jnp.logical_not(source_is_me))
        def _():
            greet((k, z))

        return 0

    lax.fori_loop(0, DP, greet_all, 0)

    def greet_dp(k, _):
        greet((lax.rem(d + k, DP), t))
        return 0

    lax.fori_loop(1, DP, greet_dp, 0)
    for device in (beside, up_y, down_y):
        greet(device)
    pl.semaphore_wait(barrier, DP + DP - 1 + DP + 3 - jnp.where(at_home, 2, 0))

    def spread(k, _):
        other = spread_to(k)
        quarter, share = k // TENSOR, lax.rem(k, TENSOR)
        src = tokens.at[pl.ds(pl.multiple_of(share * SHARE, SHARE), SHARE), pl.ds(pl.multiple_of(quarter * ROWS, ROWS), ROWS)]
        dst = tok.at[share // 4, lax.rem(share, 4), d]
        mine = jnp.logical_and(other[0] == d, other[1] == t)

        @pl.when(jnp.logical_not(mine))
        def _():
            send(src, dst, s_t1, r_t1.at[z], other)

        @pl.when(mine)
        def _():
            pltpu.make_async_copy(src, dst, r_t1.at[z]).start()

        return 0

    lax.fori_loop(0, DP, spread, 0)

    own_row = pltpu.make_async_copy(act, listed_v.at[d], l_act)
    own_row.start()

    def tell(k, _):
        send(act, listed_v.at[d], s_act, r_act, (lax.rem(d + k, DP), t))
        return 0

    lax.fori_loop(1, DP, tell, 0)

    order = [plane(k) for k in (4, 3, -3, 2, -2, 1, -1, 0)]

    def four(zq):
        return pl.ds(zq * 4, 4)

    def stage_x(o):
        mine = tok.at[xl, y, four(order[o])]
        wait(mine, r_t1.at[order[o]])
        send(mine, mine, s_x, r_x.at[o], beside)

    def stage_y(o):
        wait(tok.at[1 - xl, y, four(order[o])], r_x.at[o])
        both = tok.at[:, y, four(order[o])]
        send(both, both, s_y, r_y.at[0, o], up_y)
        send(both, both, s_y, r_y.at[1, o], down_y)

    def stage_f(o):
        first, second = pl.ds(order[o] * 4, 2), pl.ds(order[o] * 4 + 2, 2)
        wait(tok.at[:, y_last, four(order[o])], r_y.at[0, o])
        send(tok.at[:, y_last, first], tok.at[:, y_last, first], s_f, r_f.at[0, o], up_y)
        wait(tok.at[:, y_next, four(order[o])], r_y.at[1, o])
        send(tok.at[:, y_next, second], tok.at[:, y_next, second], s_f, r_f.at[1, o], down_y)

    def tile_weights(q):
        picked = [listed[q, 0, k] for k in range(CAP)]
        return jnp.concatenate([ref[b] for ref in (wg, wu) for b in picked], axis=1)

    def tile_tokens(q):
        return tok[:, :, q].reshape(TILE, ROWS)

    def partial_sum(q):
        return jnp.dot(tile_tokens(q), tile_weights(q), preferred_element_type=F32)

    def settle(o, k, received):
        total = partial_sum(order[o] * 4 + k * 2 + c)
        wait(rc.at[o, k], r_c.at[o, k])
        total = total + rc[o, k].astype(F32)
        for slot in received:
            wait(rz.at[slot, k], r_z.at[slot, k])
            total = total + rz[slot, k].astype(F32)
        return total

    def stage_c(o):
        wait(tok.at[:, y_far, pl.ds(order[o] * 4, 2)], r_f.at[0, o])
        wait(tok.at[:, y_far, pl.ds(order[o] * 4 + 2, 2)], r_f.at[1, o])

        def for_sibling(k, _):
            sc[o, k] = partial_sum(order[o] * 4 + k * 2 + 1 - c).astype(BF16)
            send(sc.at[o, k], rc.at[o, k], s_c, r_c.at[o, k], sibling)
            return 0

        lax.fori_loop(0, 2, for_sibling, 0)
        if o == 0:
            for k, slot, device in ((0, 0, up_z), (1, 1, down_z)):
                sz[o, k] = settle(o, k, ()).astype(BF16)
                send(sz.at[o, k], rz.at[slot, k], s_z, r_z.at[slot, k], device)
        elif o <= 2:
            device = up_z if o == 1 else down_z
            for k in (o - 1, 2 - o):
                sz[o, k] = settle(o, k, (o - 1,) if k == o - 1 else ()).astype(BF16)
                send(sz.at[o, k], rz.at[o + 1, k], s_z, r_z.at[o + 1, k], device)
        elif o <= 6:
            device = up_z if o % 2 else down_z

            def along(k, _):
                sz[o, k] = settle(o, k, (o - 1,)).astype(BF16)
                send(sz.at[o, k], rz.at[o + 1, k], s_z, r_z.at[o + 1, k], device)
                return 0

            lax.fori_loop(0, 2, along, 0)
        else:
            xs[...] = settle(o, 1 - xh, (6, 7)).astype(BF16)
            send(xs, xr, s_h, r_h, across)
            acc[...] = settle(o, xh, (6, 7))

    for o in range(NZ):
        stage_x(o)
        if o == 0:
            wait(wg, s_w.at[0])
            wait(wu, s_w.at[1])
            own_row.wait()
            wait(listed_v.at[pl.ds(0, DP - 1)], r_act)
            to_smem = pltpu.make_async_copy(listed_v, listed, l_act)
            to_smem.start()
            to_smem.wait()
    for o in range(3):
        stage_y(o)
    stage_f(0)
    for o in range(NZ):
        if o + 3 < NZ:
            stage_y(o + 3)
        if o + 1 < NZ:
            stage_f(o + 1)
        stage_c(o)

    wait(xr, r_h)
    both = acc[...] + xr[...].astype(F32)
    gate, up = both[:, : CAP * BLOCK], both[:, CAP * BLOCK :]
    g = live_grad[...].astype(F32)
    relu = jnp.maximum(gate, 0.0)
    gr[d, :, : CAP * BLOCK] = (g * up * 2.0 * relu).astype(BF16)
    gr[d, :, CAP * BLOCK :] = (g * relu * relu).astype(BF16)

    def own(zq, k):
        return gr.at[zq * 4 + k * 2 + c]

    def pass_on(zq, k, direction, distance):
        tile = own(zq, k)
        send(tile, tile, s_gz, r_gz.at[direction, distance, k], up_z if direction == 0 else down_z)

    def to_sibling(e, zq, k):
        tile = own(zq, k)
        send(tile, tile, s_gc, r_gc.at[e, k], sibling)

    send(gr.at[d], gr.at[d], s_gh, r_gh, across)
    pass_on(z, xh, 0, 0)
    pass_on(z, xh, 1, 0)
    to_sibling(0, z, xh)
    wait(own(z, 1 - xh), r_gh)
    pass_on(z, 1 - xh, 0, 0)
    pass_on(z, 1 - xh, 1, 0)
    to_sibling(0, z, 1 - xh)

    arrivals = [plane(k) for k in (0, -1, 1, -2, 2, -3, 3, 4)]

    def arrive(distance):
        for k in (0, 1):
            for direction in (0, 1):
                e = 1 + 2 * distance + direction
                zq = arrivals[e]
                wait(own(zq, k), r_gz.at[direction, distance, k])
                if distance < 2 or k == direction:
                    pass_on(zq, k, direction, distance + 1)
                to_sibling(e, zq, k)

    def arrive_last():
        for k in (0, 1):
            wait(own(arrivals[7], k), r_gz.at[k, 3, k])
            to_sibling(7, arrivals[7], k)

    def backward(e):
        zq = arrivals[e]
        for k in (0, 1):
            wait(gr.at[zq * 4 + k * 2 + 1 - c], r_gc.at[e, k])

        def one(k, _):
            q = zq * 4 + k
            grads = gr[q]
            value = lax.dot_general(grads, tile_weights(q), (((1,), (1,)), ((), ())), preferred_element_type=F32)
            part[:, :, q] = value.astype(BF16).reshape(2, 4, SHARE, ROWS)
            value = lax.dot_general(tile_tokens(q), grads, (((0,), (0,)), ((), ())), preferred_element_type=F32)
            piece[q] = value.astype(BF16)
            return 0

        lax.fori_loop(0, 4, one, 0)
        pltpu.make_async_copy(piece.at[four(zq)], pieces_hbm.at[four(zq)], s_p).start()
        first, second = pl.ds(zq * 4, 2), pl.ds(zq * 4 + 2, 2)
        send(part.at[:, y_far, first], yr1.at[0, e], s_0, r_0.at[0, e], up_y)
        send(part.at[:, y_far, second], yr1.at[1, e], s_0, r_0.at[1, e], down_y)

    def reduce_1(e):
        zq = arrivals[e]
        for direction, y_to, device in ((0, y_next, up_y), (1, y_last, down_y)):
            wait(yr1.at[direction, e], r_0.at[direction, e])
            half = pl.ds(zq * 4 + 2 * direction, 2)
            part[:, y_to, half] = (part[:, y_to, half].astype(F32) + yr1[direction, e].astype(F32)).astype(BF16)
            send(part.at[:, y_to, four(zq)], yr2.at[direction, e], s_1, r_1.at[direction, e], device)

    def reduce_2(e):
        zq = arrivals[e]
        for direction in (0, 1):
            wait(yr2.at[direction, e], r_1.at[direction, e])
        total = part[:, y, four(zq)].astype(F32) + yr2[0, e].astype(F32) + yr2[1, e].astype(F32)
        part[:, y, four(zq)] = total.astype(BF16)
        send(part.at[1 - xl, y, four(zq)], xr2.at[e], s_2, r_2.at[e], beside)

    def reduce_3(e):
        zq = arrivals[e]
        wait(xr2.at[e], r_2.at[e])
        fin[four(zq)] = (part[xl, y, four(zq)].astype(F32) + xr2[e].astype(F32)).astype(BF16)

        def home(k, _):
            q = zq * 4 + k
            dst = out.at[pl.ds(pl.multiple_of(t * SHARE, SHARE), SHARE), pl.ds(pl.multiple_of(a * ROWS, ROWS), ROWS)]
            mine = jnp.logical_and(q == d, at_home)

            @pl.when(jnp.logical_not(mine))
            def _():
                send(fin.at[q], dst, s_o, r_o, (q, z))

            @pl.when(mine)
            def _():
                pltpu.make_async_copy(fin.at[q], dst, r_o).start()

            return 0

        lax.fori_loop(0, 4, home, 0)

    for e in range(NZ + 3):
        if e == 1 or e == 3 or e == 5:
            arrive(e // 2)
        if e == 7:
            arrive_last()
        if e < NZ:
            backward(e)
        if 0 <= e - 1 < NZ:
            reduce_1(e - 1)
        if 0 <= e - 2 < NZ:
            reduce_2(e - 2)
        if 0 <= e - 3 < NZ:
            reduce_3(e - 3)

    wait(out, r_o)

    for sem in (s_t1, s_o):

        @pl.when(at_home)
        def _():
            wait(fin.at[pl.ds(0, DP - 1)], sem)

        @pl.when(jnp.logical_not(at_home))
        def _():
            wait(fin, sem)

    wait(listed_v.at[pl.ds(0, DP - 1)], s_act)
    wait(fin, s_x)
    wait(tok.at[0], s_y)
    wait(tok.at[0, pl.ds(0, 2)], s_f)
    wait(sc, s_c)
    wait(sz, s_z)
    wait(xs, s_h)
    wait(gr.at[d], s_gh)
    wait(gr.at[pl.ds(0, 14)], s_gz)
    wait(gr.at[pl.ds(0, 16)], s_gc)
    wait(yr1, s_0)
    wait(yr2, s_1)
    wait(xr2, s_2)
    wait(piece, s_p)


def sum_kernel(listed, piece_ref, dgate_ref, dup_ref, gate_acc, up_acc):
    step = pl.program_id(0)
    tiles = piece_ref.shape[0]

    @pl.when(step == 0)
    def _():
        gate_acc[...] = jnp.zeros_like(gate_acc)
        up_acc[...] = jnp.zeros_like(up_acc)

    for k in range(tiles):
        for c in range(CAP):
            block = listed[step * tiles + k, 0, c]
            at = pl.ds(pl.multiple_of(block * BLOCK, BLOCK), BLOCK)
            for m, acc in enumerate((gate_acc, up_acc)):
                column = (m * CAP + c) * BLOCK
                acc[:, at] += piece_ref[k, :, column : column + BLOCK].astype(F32)

    @pl.when(step == pl.num_programs(0) - 1)
    def _():
        dgate_ref[...] = gate_acc[...].astype(BF16)
        dup_ref[...] = up_acc[...].astype(BF16)


def per_device(tokens, out_grad, active, w_gate, w_up):
    width = w_gate.shape[1]
    blocks = width // BLOCK
    act = jnp.pad(jnp.minimum(active.reshape(1, CAP), blocks - 1), ((0, 0), (0, BLOCK - CAP)))
    live = jnp.repeat(active.reshape(1, CAP) < blocks, BLOCK, axis=1)
    live_grad = jnp.where(live, out_grad.reshape(TILE, CAP * BLOCK), 0)
    vmem = pl.BlockSpec(memory_space=pltpu.VMEM)
    anywhere = pl.BlockSpec(memory_space=pl.ANY)
    dma, v = pltpu.SemaphoreType.DMA, pltpu.VMEM
    tile = (TILE, UNITS)
    slab = (SHARE, ROWS)
    input_grad, pieces, listed = pl.pallas_call(
        main_kernel,
        in_specs=[vmem, vmem, vmem, anywhere, anywhere],
        out_specs=[vmem, anywhere, pl.BlockSpec(memory_space=pltpu.SMEM)],
        out_shape=[
            jax.ShapeDtypeStruct((TILE, QUARTERS * ROWS), BF16),
            jax.ShapeDtypeStruct((DP, ROWS, UNITS), BF16),
            jax.ShapeDtypeStruct((DP, 1, BLOCK), jnp.int32),
        ],
        scratch_shapes=[
            v((blocks, ROWS, BLOCK), BF16),
            v((blocks, ROWS, BLOCK), BF16),
            v((DP, 1, BLOCK), jnp.int32),
            v((2, 4, DP, *slab), BF16),
            v((NZ, 2, *tile), BF16),
            v((NZ, 2, *tile), BF16),
            v((NZ - 1, 2, *tile), BF16),
            v((NZ, 2, *tile), BF16),
            v(tile, BF16),
            v(tile, BF16),
            v(tile, F32),
            v((DP, *tile), BF16),
            v((2, 4, DP, *slab), BF16),
            v((DP, ROWS, UNITS), BF16),
            v((2, NZ, 2, 2, *slab), BF16),
            v((2, NZ, 2, 4, *slab), BF16),
            v((NZ, 4, *slab), BF16),
            v((DP, *slab), BF16),
            dma, dma((NZ,)), dma, dma, dma, dma((2,)),
            dma, dma((NZ,)), dma, dma((2, NZ)), dma, dma((2, NZ)),
            dma, dma((NZ, 2)), dma, dma((NZ, 2)), dma, dma,
            dma, dma, dma, dma((2, 4, 2)), dma, dma((NZ, 2)),
            dma, dma((2, NZ)), dma, dma((2, NZ)), dma, dma((NZ,)),
            dma, dma, dma,
        ],
        compiler_params=pltpu.CompilerParams(
            collective_id=0, has_side_effects=True, vmem_limit_bytes=62 * 2**20
        ),
    )(tokens, live_grad, act, w_gate, w_up)

    tiles = 4
    whole = pl.BlockSpec((ROWS, width), lambda q, *_: (0, 0))
    dgate, dup = pl.pallas_call(
        sum_kernel,
        grid_spec=pltpu.PrefetchScalarGridSpec(
            num_scalar_prefetch=1,
            grid=(DP // tiles,),
            in_specs=[pl.BlockSpec((tiles, ROWS, UNITS), lambda q, *_: (q, 0, 0))],
            out_specs=[whole, whole],
            scratch_shapes=[v((ROWS, width), F32)] * 2,
        ),
        out_shape=[jax.ShapeDtypeStruct((ROWS, width), BF16)] * 2,
        compiler_params=pltpu.CompilerParams(vmem_limit_bytes=40 * 2**20),
    )(listed, pieces)
    return input_grad, dgate, dup


def solution(mesh):
    placed = (
        P("dp", "tensor"),
        P("dp", "tensor", None),
        P("dp", "tensor", None),
        P("dp", "tensor"),
        P("dp", "tensor"),
    )
    return jax.shard_map(
        per_device,
        mesh=mesh,
        in_specs=placed,
        out_specs=(P("dp", "tensor"), P("dp", "tensor"), P("dp", "tensor")),
        check_vma=False,
    )
```

```python
import jax
import jax.numpy as jnp
from jax import lax
from jax.experimental import pallas as pl
from jax.experimental.pallas import tpu as pltpu
from jax.sharding import PartitionSpec as P

MESH = pl.DeviceIdType.MESH
BLOCK, TILE, CAP = 128, 256, 2
NZ, QUARTERS, TENSOR, DP = 8, 4, 8, 32
ROWS = 256
SHARE = TILE // TENSOR
UNITS = 2 * CAP * BLOCK
BF16, F32 = jnp.bfloat16, jnp.float32


def send(src, dst, send_sem, recv_sem, device):
    pltpu.make_async_remote_copy(
        src_ref=src, dst_ref=dst, send_sem=send_sem, recv_sem=recv_sem, device_id=device, device_id_type=MESH
    ).start()


def wait(ref, sem):
    pltpu.make_async_copy(ref, ref, sem).wait()


def main_kernel(
    tokens, out_grad, live, act, wg_hbm, wu_hbm,
    out, pieces_hbm, listed,
    wg, wu, listed_v, tok, sc, rc, sz, rz, xs, xr, acc, gr, part, piece, yr1, yr2, xr2, fin, ts, back,
    s_t1, r_t1, s_act, r_act, l_act, s_w, s_x, r_x, s_y, r_y, s_f, r_f, s_c, r_c, s_z, r_z, s_h, r_h,
    s_gh, r_gh, s_gz, r_gz, s_gc, r_gc, s_0, r_0, s_1, r_1, s_2, r_2, s_o, r_o, s_p, s_ts, r_ts, s_out, r_out,
):
    d, t = lax.axis_index("dp"), lax.axis_index("tensor")
    z, a = d // QUARTERS, lax.rem(d, QUARTERS)
    xh, c = a // 2, lax.rem(a, 2)
    xl, y = t // 4, lax.rem(t, 4)

    def plane(dz):
        return lax.rem(z + dz + NZ, NZ)

    up_z, down_z = (plane(1) * 4 + a, t), (plane(-1) * 4 + a, t)
    sibling = (d + 1 - 2 * c, t)
    across = (z * 4 + (1 - xh) * 2 + c, t)
    beside = (d, (1 - xl) * 4 + y)
    y_next, y_last, y_far = lax.rem(y + 1, 4), lax.rem(y + 3, 4), lax.rem(y + 2, 4)
    up_y, down_y = (d, xl * 4 + y_next), (d, xl * 4 + y_last)

    def load_block(b, _):
        columns = pl.ds(pl.multiple_of(b * BLOCK, BLOCK), BLOCK)
        pltpu.make_async_copy(wg_hbm.at[:, columns], wg.at[b], s_w.at[0]).start()
        pltpu.make_async_copy(wu_hbm.at[:, columns], wu.at[b], s_w.at[1]).start()
        return 0

    lax.fori_loop(0, wg.shape[0], load_block, 0)

    barrier = pltpu.get_barrier_semaphore()

    def greet(device):
        pl.semaphore_signal(barrier, inc=1, device_id=device, device_id_type=MESH)

    def greet_dp(k, _):
        greet((lax.rem(d + k, DP), t))
        return 0

    def greet_plane(k, _):
        greet((d, lax.rem(t + k, TENSOR)))
        return 0

    lax.fori_loop(1, TENSOR, greet_plane, 0)
    lax.fori_loop(1, DP, greet_dp, 0)
    pl.semaphore_wait(barrier, TENSOR - 1 + DP - 1)

    def share_rows(s):
        return pl.ds(pl.multiple_of(s * SHARE, SHARE), SHARE)

    def to_plane(k, _):
        s = lax.rem(t + k, TENSOR)
        send(tokens.at[share_rows(s)], ts.at[t], s_ts, r_ts.at[t], (d, s))
        return 0

    pltpu.make_async_copy(tokens.at[share_rows(t)], ts.at[t], r_ts.at[t]).start()
    lax.fori_loop(1, TENSOR, to_plane, 0)

    own_row = pltpu.make_async_copy(act, listed_v.at[d], l_act)
    own_row.start()

    def tell(k, _):
        send(act, listed_v.at[d], s_act, r_act, (lax.rem(d + k, DP), t))
        return 0

    lax.fori_loop(1, DP, tell, 0)

    def quarter_columns(k):
        return pl.ds(pl.multiple_of(k * ROWS, ROWS), ROWS)

    def to_rows(far):
        wait(ts.at[far], r_ts.at[far])

        def one(k, _):
            other = far * QUARTERS + k

            @pl.when(other != d)
            def _():
                send(ts.at[far, :, quarter_columns(k)], tok.at[xl, y, d], s_t1, r_t1.at[z], (other, t))

            @pl.when(other == d)
            def _():
                pltpu.make_async_copy(ts.at[far, :, quarter_columns(k)], tok.at[xl, y, d], r_t1.at[z]).start()

            return 0

        lax.fori_loop(0, QUARTERS, one, 0)

    for k in (4, -3, 3, -2, 2, -1, 1, 0):
        to_rows(plane(k))

    order = [plane(k) for k in (4, 3, -3, 2, -2, 1, -1, 0)]

    def four(zq):
        return pl.ds(zq * 4, 4)

    def stage_x(o):
        mine = tok.at[xl, y, four(order[o])]
        wait(mine, r_t1.at[order[o]])
        send(mine, mine, s_x, r_x.at[o], beside)

    def stage_y(o):
        wait(tok.at[1 - xl, y, four(order[o])], r_x.at[o])
        both = tok.at[:, y, four(order[o])]
        send(both, both, s_y, r_y.at[0, o], up_y)
        send(both, both, s_y, r_y.at[1, o], down_y)

    def stage_f(o):
        first, second = pl.ds(order[o] * 4, 2), pl.ds(order[o] * 4 + 2, 2)
        wait(tok.at[:, y_last, four(order[o])], r_y.at[0, o])
        send(tok.at[:, y_last, first], tok.at[:, y_last, first], s_f, r_f.at[0, o], up_y)
        wait(tok.at[:, y_next, four(order[o])], r_y.at[1, o])
        send(tok.at[:, y_next, second], tok.at[:, y_next, second], s_f, r_f.at[1, o], down_y)

    def tile_weights(q):
        picked = [listed[q, 0, k] for k in range(CAP)]
        return jnp.concatenate([ref[b] for ref in (wg, wu) for b in picked], axis=1)

    def tile_tokens(q):
        return tok[:, :, q].reshape(TILE, ROWS)

    def partial_sum(q):
        return jnp.dot(tile_tokens(q), tile_weights(q), preferred_element_type=F32)

    def settle(o, k, received):
        total = partial_sum(order[o] * 4 + k * 2 + c)
        wait(rc.at[o, k], r_c.at[o, k])
        total = total + rc[o, k].astype(F32)
        for slot in received:
            wait(rz.at[slot, k], r_z.at[slot, k])
            total = total + rz[slot, k].astype(F32)
        return total

    def stage_c(o):
        wait(tok.at[:, y_far, pl.ds(order[o] * 4, 2)], r_f.at[0, o])
        wait(tok.at[:, y_far, pl.ds(order[o] * 4 + 2, 2)], r_f.at[1, o])

        def for_sibling(k, _):
            sc[o, k] = partial_sum(order[o] * 4 + k * 2 + 1 - c).astype(BF16)
            send(sc.at[o, k], rc.at[o, k], s_c, r_c.at[o, k], sibling)
            return 0

        lax.fori_loop(0, 2, for_sibling, 0)
        if o == 0:
            for k, slot, device in ((0, 0, up_z), (1, 1, down_z)):
                sz[o, k] = settle(o, k, ()).astype(BF16)
                send(sz.at[o, k], rz.at[slot, k], s_z, r_z.at[slot, k], device)
        elif o <= 2:
            device = up_z if o == 1 else down_z
            for k in (o - 1, 2 - o):
                sz[o, k] = settle(o, k, (o - 1,) if k == o - 1 else ()).astype(BF16)
                send(sz.at[o, k], rz.at[o + 1, k], s_z, r_z.at[o + 1, k], device)
        elif o <= 6:
            device = up_z if o % 2 else down_z

            def along(k, _):
                sz[o, k] = settle(o, k, (o - 1,)).astype(BF16)
                send(sz.at[o, k], rz.at[o + 1, k], s_z, r_z.at[o + 1, k], device)
                return 0

            lax.fori_loop(0, 2, along, 0)
        else:
            xs[...] = settle(o, 1 - xh, (6, 7)).astype(BF16)
            send(xs, xr, s_h, r_h, across)
            acc[...] = settle(o, xh, (6, 7))

    for o in range(NZ):
        stage_x(o)
        if o == 0:
            wait(wg, s_w.at[0])
            wait(wu, s_w.at[1])
            own_row.wait()
            wait(listed_v.at[pl.ds(0, DP - 1)], r_act)
            to_smem = pltpu.make_async_copy(listed_v, listed, l_act)
            to_smem.start()
            to_smem.wait()
    for o in range(3):
        stage_y(o)
    stage_f(0)
    for o in range(NZ):
        if o + 3 < NZ:
            stage_y(o + 3)
        if o + 1 < NZ:
            stage_f(o + 1)
        stage_c(o)

    wait(xr, r_h)
    both = acc[...] + xr[...].astype(F32)
    gate, up = both[:, : CAP * BLOCK], both[:, CAP * BLOCK :]
    g = out_grad[...].astype(F32) * live[...]
    relu = jnp.maximum(gate, 0.0)
    gr[d, :, : CAP * BLOCK] = (g * up * 2.0 * relu).astype(BF16)
    gr[d, :, CAP * BLOCK :] = (g * relu * relu).astype(BF16)

    def own(zq, k):
        return gr.at[zq * 4 + k * 2 + c]

    def pass_on(zq, k, direction, distance):
        tile = own(zq, k)
        send(tile, tile, s_gz, r_gz.at[direction, distance, k], up_z if direction == 0 else down_z)

    def to_sibling(e, zq, k):
        tile = own(zq, k)
        send(tile, tile, s_gc, r_gc.at[e, k], sibling)

    send(gr.at[d], gr.at[d], s_gh, r_gh, across)
    pass_on(z, xh, 0, 0)
    pass_on(z, xh, 1, 0)
    to_sibling(0, z, xh)
    wait(own(z, 1 - xh), r_gh)
    pass_on(z, 1 - xh, 0, 0)
    pass_on(z, 1 - xh, 1, 0)
    to_sibling(0, z, 1 - xh)

    arrivals = [plane(k) for k in (0, -1, 1, -2, 2, -3, 3, 4)]

    def arrive(distance):
        for k in (0, 1):
            for direction in (0, 1):
                e = 1 + 2 * distance + direction
                zq = arrivals[e]
                wait(own(zq, k), r_gz.at[direction, distance, k])
                if distance < 2 or k == direction:
                    pass_on(zq, k, direction, distance + 1)
                to_sibling(e, zq, k)

    def arrive_last():
        for k in (0, 1):
            wait(own(arrivals[7], k), r_gz.at[k, 3, k])
            to_sibling(7, arrivals[7], k)

    def backward(e):
        zq = arrivals[e]
        for k in (0, 1):
            wait(gr.at[zq * 4 + k * 2 + 1 - c], r_gc.at[e, k])

        def one(k, _):
            q = zq * 4 + k
            grads = gr[q]
            value = lax.dot_general(grads, tile_weights(q), (((1,), (1,)), ((), ())), preferred_element_type=F32)
            part[:, :, q] = value.astype(BF16).reshape(2, 4, SHARE, ROWS)
            value = lax.dot_general(tile_tokens(q), grads, (((0,), (0,)), ((), ())), preferred_element_type=F32)
            piece[q] = value.astype(BF16)
            return 0

        lax.fori_loop(0, 4, one, 0)
        pltpu.make_async_copy(piece.at[four(zq)], pieces_hbm.at[four(zq)], s_p).start()
        first, second = pl.ds(zq * 4, 2), pl.ds(zq * 4 + 2, 2)
        send(part.at[:, y_far, first], yr1.at[0, e], s_0, r_0.at[0, e], up_y)
        send(part.at[:, y_far, second], yr1.at[1, e], s_0, r_0.at[1, e], down_y)

    def reduce_1(e):
        zq = arrivals[e]
        for direction, y_to, device in ((0, y_next, up_y), (1, y_last, down_y)):
            wait(yr1.at[direction, e], r_0.at[direction, e])
            half = pl.ds(zq * 4 + 2 * direction, 2)
            part[:, y_to, half] = (part[:, y_to, half].astype(F32) + yr1[direction, e].astype(F32)).astype(BF16)
            send(part.at[:, y_to, four(zq)], yr2.at[direction, e], s_1, r_1.at[direction, e], device)

    def reduce_2(e):
        zq = arrivals[e]
        for direction in (0, 1):
            wait(yr2.at[direction, e], r_1.at[direction, e])
        total = part[:, y, four(zq)].astype(F32) + yr2[0, e].astype(F32) + yr2[1, e].astype(F32)
        part[:, y, four(zq)] = total.astype(BF16)
        send(part.at[1 - xl, y, four(zq)], xr2.at[e], s_2, r_2.at[e], beside)

    def reduce_3(e):
        zq = arrivals[e]
        wait(xr2.at[e], r_2.at[e])
        fin[four(zq)] = (part[xl, y, four(zq)].astype(F32) + xr2[e].astype(F32)).astype(BF16)

        def home(k, _):
            q = zq * 4 + k
            dst = back.at[z, :, quarter_columns(a)]

            @pl.when(q != d)
            def _():
                send(fin.at[q], dst, s_o, r_o.at[z], (q, t))

            @pl.when(q == d)
            def _():
                pltpu.make_async_copy(fin.at[q], dst, r_o.at[z]).start()

            return 0

        lax.fori_loop(0, 4, home, 0)

    def to_owner(e):
        far = plane((0, 1, -1, 2, -2, 3, -3, 4)[e])
        wait(back.at[far], r_o.at[far])
        dst = out.at[share_rows(t)]

        @pl.when(far != t)
        def _():
            send(back.at[far], dst, s_out, r_out, (d, far))

        @pl.when(far == t)
        def _():
            pltpu.make_async_copy(back.at[far], dst, r_out).start()

    backward(0)
    reduce_1(0)
    arrive(0)
    backward(1), backward(2)
    reduce_2(0)
    reduce_1(1), reduce_1(2)
    arrive(1)
    backward(3), backward(4)
    reduce_3(0), reduce_2(1), reduce_2(2)
    reduce_1(3), reduce_1(4)
    arrive(2)
    backward(5), backward(6)
    reduce_3(1), reduce_3(2), reduce_2(3), reduce_2(4), to_owner(0)
    reduce_1(5)
    arrive_last()
    backward(7)
    reduce_1(6)
    reduce_3(3), reduce_3(4), reduce_2(5)
    reduce_1(7)
    reduce_2(6), to_owner(1), to_owner(2)
    reduce_2(7)
    reduce_3(5), reduce_3(6), reduce_3(7)
    for e in range(3, NZ):
        to_owner(e)

    wait(out, r_out)

    wait(fin.at[pl.ds(0, DP - 1)], s_t1)
    wait(fin.at[pl.ds(0, DP - 1)], s_o)
    wait(ts.at[pl.ds(0, TENSOR - 1)], s_ts)
    wait(ts.at[pl.ds(0, TENSOR - 1)], s_out)
    wait(listed_v.at[pl.ds(0, DP - 1)], s_act)
    wait(fin, s_x)
    wait(tok.at[0], s_y)
    wait(tok.at[0, pl.ds(0, 2)], s_f)
    wait(sc, s_c)
    wait(sz, s_z)
    wait(xs, s_h)
    wait(gr.at[d], s_gh)
    wait(gr.at[pl.ds(0, 14)], s_gz)
    wait(gr.at[pl.ds(0, 16)], s_gc)
    wait(yr1, s_0)
    wait(yr2, s_1)
    wait(xr2, s_2)
    wait(piece, s_p)


def sum_kernel(listed, piece_ref, dgate_ref, dup_ref, gate_acc, up_acc):
    step = pl.program_id(0)
    tiles = piece_ref.shape[0]

    @pl.when(step == 0)
    def _():
        gate_acc[...] = jnp.zeros_like(gate_acc)
        up_acc[...] = jnp.zeros_like(up_acc)

    for k in range(tiles):
        for c in range(CAP):
            block = listed[step * tiles + k, 0, c]
            at = pl.ds(pl.multiple_of(block * BLOCK, BLOCK), BLOCK)
            for m, acc in enumerate((gate_acc, up_acc)):
                column = (m * CAP + c) * BLOCK
                acc[:, at] += piece_ref[k, :, column : column + BLOCK].astype(F32)

    @pl.when(step == pl.num_programs(0) - 1)
    def _():
        dgate_ref[...] = gate_acc[...].astype(BF16)
        dup_ref[...] = up_acc[...].astype(BF16)


def per_device(tokens, out_grad, active, w_gate, w_up):
    width = w_gate.shape[1]
    blocks = width // BLOCK
    act = jnp.pad(jnp.minimum(active.reshape(1, CAP), blocks - 1), ((0, 0), (0, BLOCK - CAP)))
    live = jnp.repeat(active.reshape(1, CAP) < blocks, BLOCK, axis=1).astype(F32)
    vmem = pl.BlockSpec(memory_space=pltpu.VMEM)
    anywhere = pl.BlockSpec(memory_space=pl.ANY)
    dma, v = pltpu.SemaphoreType.DMA, pltpu.VMEM
    tile = (TILE, UNITS)
    slab = (SHARE, ROWS)
    input_grad, pieces, listed = pl.pallas_call(
        main_kernel,
        in_specs=[vmem, vmem, vmem, vmem, anywhere, anywhere],
        out_specs=[vmem, anywhere, pl.BlockSpec(memory_space=pltpu.SMEM)],
        out_shape=[
            jax.ShapeDtypeStruct((TILE, QUARTERS * ROWS), BF16),
            jax.ShapeDtypeStruct((DP, ROWS, UNITS), BF16),
            jax.ShapeDtypeStruct((DP, 1, BLOCK), jnp.int32),
        ],
        scratch_shapes=[
            v((blocks, ROWS, BLOCK), BF16),
            v((blocks, ROWS, BLOCK), BF16),
            v((DP, 1, BLOCK), jnp.int32),
            v((2, 4, DP, *slab), BF16),
            v((NZ, 2, *tile), BF16),
            v((NZ, 2, *tile), BF16),
            v((NZ - 1, 2, *tile), BF16),
            v((NZ, 2, *tile), BF16),
            v(tile, BF16),
            v(tile, BF16),
            v(tile, F32),
            v((DP, *tile), BF16),
            v((2, 4, DP, *slab), BF16),
            v((DP, ROWS, UNITS), BF16),
            v((2, NZ, 2, 2, *slab), BF16),
            v((2, NZ, 2, 4, *slab), BF16),
            v((NZ, 4, *slab), BF16),
            v((DP, *slab), BF16),
            v((TENSOR, SHARE, QUARTERS * ROWS), BF16),
            v((TENSOR, SHARE, QUARTERS * ROWS), BF16),
            dma, dma((NZ,)), dma, dma, dma, dma((2,)),
            dma, dma((NZ,)), dma, dma((2, NZ)), dma, dma((2, NZ)),
            dma, dma((NZ, 2)), dma, dma((NZ, 2)), dma, dma,
            dma, dma, dma, dma((2, 4, 2)), dma, dma((NZ, 2)),
            dma, dma((2, NZ)), dma, dma((2, NZ)), dma, dma((NZ,)),
            dma, dma((NZ,)), dma,
            dma, dma((NZ,)), dma, dma,
        ],
        compiler_params=pltpu.CompilerParams(
            collective_id=0, has_side_effects=True, vmem_limit_bytes=62 * 2**20
        ),
    )(tokens, out_grad.reshape(TILE, CAP * BLOCK), live, act, w_gate, w_up)

    tiles = 4
    whole = pl.BlockSpec((ROWS, width), lambda q, *_: (0, 0))
    dgate, dup = pl.pallas_call(
        sum_kernel,
        grid_spec=pltpu.PrefetchScalarGridSpec(
            num_scalar_prefetch=1,
            grid=(DP // tiles,),
            in_specs=[pl.BlockSpec((tiles, ROWS, UNITS), lambda q, *_: (q, 0, 0))],
            out_specs=[whole, whole],
            scratch_shapes=[v((ROWS, width), F32)] * 2,
        ),
        out_shape=[jax.ShapeDtypeStruct((ROWS, width), BF16)] * 2,
        compiler_params=pltpu.CompilerParams(vmem_limit_bytes=60 * 2**20),
    )(listed, pieces)
    return input_grad, dgate, dup


def solution(mesh):
    placed = (
        P("dp", "tensor"),
        P("dp", "tensor", None),
        P("dp", "tensor", None),
        P("dp", "tensor"),
        P("dp", "tensor"),
    )
    return jax.shard_map(
        per_device,
        mesh=mesh,
        in_specs=placed,
        out_specs=(P("dp", "tensor"), P("dp", "tensor"), P("dp", "tensor")),
        check_vma=False,
    )
```

```python
import jax
import jax.numpy as jnp
from jax import lax
from jax.experimental import pallas as pl
from jax.experimental.pallas import tpu as pltpu
from jax.sharding import PartitionSpec as P

MESH = pl.DeviceIdType.MESH
BLOCK, TILE, CAP = 128, 256, 2
NZ, QUARTERS, TENSOR, DP = 8, 4, 8, 32
ROWS = 256
SHARE = TILE // TENSOR
UNITS = 2 * CAP * BLOCK
HALF = UNITS // 2
BF16, F32 = jnp.bfloat16, jnp.float32


def send(src, dst, send_sem, recv_sem, device):
    pltpu.make_async_remote_copy(
        src_ref=src, dst_ref=dst, send_sem=send_sem, recv_sem=recv_sem, device_id=device, device_id_type=MESH
    ).start()


def wait(ref, sem):
    pltpu.make_async_copy(ref, ref, sem).wait()


def main_kernel(
    tokens, out_grad, live, act, wg_hbm, wu_hbm,
    out, pieces_hbm, listed,
    wg, wu, listed_v, tok, sc, rc, sza, rza, szb, rzb, xb_s, xb_r, ch, xs, xr, gr, part, piece, yr1, yr2, xr2, fin, ts, back,
    s_t1, r_t1, s_act, r_act, l_act, s_w, s_x, r_x, s_y, r_y, s_f, r_f, s_c, r_c, s_za, r_za, s_zb, r_zb, s_xb, r_xb, s_h, r_h,
    s_gh, r_gh, s_gz, r_gz, s_gc, r_gc, s_0, r_0, s_1, r_1, s_2, r_2, s_o, r_o, s_p, s_ts, r_ts, s_out, r_out, s_x0, r_x0,
):
    d, t = lax.axis_index("dp"), lax.axis_index("tensor")
    z, a = d // QUARTERS, lax.rem(d, QUARTERS)
    xh, c = a // 2, lax.rem(a, 2)
    xl, y = t // 4, lax.rem(t, 4)

    def plane(dz):
        return lax.rem(z + dz + NZ, NZ)

    up_z, down_z = (plane(1) * 4 + a, t), (plane(-1) * 4 + a, t)
    sibling = (d + 1 - 2 * c, t)
    across = (z * 4 + (1 - xh) * 2 + c, t)
    beside = (d, (1 - xl) * 4 + y)
    y_next, y_last, y_far = lax.rem(y + 1, 4), lax.rem(y + 3, 4), lax.rem(y + 2, 4)
    up_y, down_y = (d, xl * 4 + y_next), (d, xl * 4 + y_last)

    barrier = pltpu.get_barrier_semaphore()

    def greet(device):
        pl.semaphore_signal(barrier, inc=1, device_id=device, device_id_type=MESH)

    def greet_dp(k, _):
        greet((lax.rem(d + k, DP), t))
        return 0

    def greet_plane(k, _):
        greet((d, lax.rem(t + k, TENSOR)))
        return 0

    lax.fori_loop(1, TENSOR, greet_plane, 0)
    lax.fori_loop(1, DP, greet_dp, 0)
    pl.semaphore_wait(barrier, TENSOR - 1 + DP - 1)

    def share_rows(s):
        return pl.ds(pl.multiple_of(s * SHARE, SHARE), SHARE)

    def to_plane(k, _):
        s = lax.rem(t + k, TENSOR)
        send(tokens.at[share_rows(s)], ts.at[t], s_ts, r_ts.at[t], (d, s))
        return 0

    pltpu.make_async_copy(tokens.at[share_rows(t)], ts.at[t], r_ts.at[t]).start()
    lax.fori_loop(1, TENSOR, to_plane, 0)

    def quarter_columns(k):
        return pl.ds(pl.multiple_of(k * ROWS, ROWS), ROWS)

    def to_rows(far):
        wait(ts.at[far], r_ts.at[far])

        def one(k, _):
            other = far * QUARTERS + k

            @pl.when(other != d)
            def _():
                send(ts.at[far, :, quarter_columns(k)], tok.at[xl, y, d], s_t1, r_t1.at[z], (other, t))

            @pl.when(other == d)
            def _():
                pltpu.make_async_copy(ts.at[far, :, quarter_columns(k)], tok.at[xl, y, d], r_t1.at[z]).start()

            return 0

        lax.fori_loop(0, QUARTERS, one, 0)

    for k in (4, -3, 3, -2, 2, -1, 1, 0):
        to_rows(plane(k))

    own_row = pltpu.make_async_copy(act, listed_v.at[d], l_act)
    own_row.start()

    def tell(k, _):
        send(act, listed_v.at[d], s_act, r_act, (lax.rem(d + k, DP), t))
        return 0

    lax.fori_loop(1, DP, tell, 0)

    def load_block(b, _):
        columns = pl.ds(pl.multiple_of(b * BLOCK, BLOCK), BLOCK)
        pltpu.make_async_copy(wg_hbm.at[:, columns], wg.at[b], s_w.at[0]).start()
        pltpu.make_async_copy(wu_hbm.at[:, columns], wu.at[b], s_w.at[1]).start()
        return 0

    lax.fori_loop(0, wg.shape[0], load_block, 0)

    order = [plane(k) for k in (4, 3, -3, 2, -2, 1, -1, 0)]

    def four(zq):
        return pl.ds(zq * 4, 4)

    def stage_all(o):
        mine = tok.at[xl, y, four(order[o])]
        wait(mine, r_t1.at[order[o]])

        def one(k, _):
            send(mine, mine, s_x0, r_x0, (d, lax.rem(t + k, TENSOR)))
            return 0

        lax.fori_loop(1, TENSOR, one, 0)

    def stage_x(o):
        mine = tok.at[xl, y, four(order[o])]
        wait(mine, r_t1.at[order[o]])
        send(mine, mine, s_x, r_x.at[o], beside)

    def stage_y(o):
        wait(tok.at[1 - xl, y, four(order[o])], r_x.at[o])
        both = tok.at[:, y, four(order[o])]
        send(both, both, s_y, r_y.at[0, o], up_y)
        send(both, both, s_y, r_y.at[1, o], down_y)

    def stage_f(o):
        first, second = pl.ds(order[o] * 4, 2), pl.ds(order[o] * 4 + 2, 2)
        wait(tok.at[:, y_last, four(order[o])], r_y.at[0, o])
        send(tok.at[:, y_last, first], tok.at[:, y_last, first], s_f, r_f.at[0, o], up_y)
        wait(tok.at[:, y_next, four(order[o])], r_y.at[1, o])
        send(tok.at[:, y_next, second], tok.at[:, y_next, second], s_f, r_f.at[1, o], down_y)

    def tile_weights(q):
        picked = [listed[q, 0, k] for k in range(CAP)]
        return jnp.concatenate([ref[b] for ref in (wg, wu) for b in picked], axis=1)

    def tile_tokens(q):
        return tok[:, :, q].reshape(TILE, ROWS)

    def partial_sum(q):
        return jnp.dot(tile_tokens(q), tile_weights(q), preferred_element_type=F32)

    def along(o):
        return up_z if o % 2 else down_z

    def chip_sum(o):
        if o == 0:
            wait(fin.at[pl.ds(0, 4 * (TENSOR - 1))], r_x0)
        else:
            wait(tok.at[:, y_far, pl.ds(order[o] * 4, 2)], r_f.at[0, o])
            wait(tok.at[:, y_far, pl.ds(order[o] * 4 + 2, 2)], r_f.at[1, o])

        def for_sibling(k, _):
            sc[o, k] = partial_sum(order[o] * 4 + k * 2 + 1 - c).astype(BF16)
            send(sc.at[o, k], rc.at[o, k], s_c, r_c.at[o, k], sibling)
            return 0

        lax.fori_loop(0, 2, for_sibling, 0)

        def for_me(k, _):
            ch[o % 2, k] = partial_sum(order[o] * 4 + k * 2 + c)
            return 0

        lax.fori_loop(0, 2, for_me, 0)

    def join(o):
        for k in (1 - xh, xh):
            wait(rc.at[o, k], r_c.at[o, k])
            ch[o % 2, k] += rc[o, k].astype(F32)
            if k is not xh:
                xb_s[o] = ch[o % 2, k, :, HALF:].astype(BF16)
                send(xb_s.at[o], xb_r.at[o], s_xb, r_xb.at[o], across)

    def gate_sum(o, k, slots):
        total = ch[o % 2, k, :, :HALF]
        for slot in slots:
            wait(rza.at[slot, k], r_za.at[slot, k])
            total = total + rza[slot, k].astype(F32)
        return total

    def up_sum(o, slots, rows):
        total = ch[o % 2, xh, rows, HALF:] + xb_r[o, rows].astype(F32)
        for slot in slots:
            wait(rzb.at[slot, rows], r_zb.at[slot])
            total = total + rzb[slot, rows].astype(F32)
        return total

    top, bottom, full = pl.ds(0, TILE // 2), pl.ds(TILE // 2, TILE // 2), pl.ds(0, TILE)

    def ring(o):
        if o == 0:
            for k, device in ((0, up_z), (1, down_z)):
                sza[o, k] = gate_sum(o, k, ()).astype(BF16)
                send(sza.at[o, k], rza.at[k, k], s_za, r_za.at[k, k], device)
            wait(xb_r.at[o], r_xb.at[o])
            for k, device, rows in ((0, up_z, top), (1, down_z, bottom)):
                szb[o, rows] = up_sum(o, (), rows).astype(BF16)
                send(szb.at[o, rows], rzb.at[k, rows], s_zb, r_zb.at[k], device)
            return
        device, slot = along(o), o + 1
        if o <= 2:
            for k in (o - 1, 2 - o):
                sza[o, k] = gate_sum(o, k, (o - 1,) if k == o - 1 else ()).astype(BF16)
                send(sza.at[o, k], rza.at[slot, k], s_za, r_za.at[slot, k], device)
            wait(xb_r.at[o], r_xb.at[o])
            for k, rows in ((0, top), (1, bottom)):
                szb[o, rows] = up_sum(o, (o - 1,) if k == o - 1 else (), rows).astype(BF16)
            send(szb.at[o], rzb.at[slot], s_zb, r_zb.at[slot], device)
        elif o <= 6:

            def one(k, _):
                sza[o, k] = gate_sum(o, k, (o - 1,)).astype(BF16)
                send(sza.at[o, k], rza.at[slot, k], s_za, r_za.at[slot, k], device)
                return 0

            lax.fori_loop(0, 2, one, 0)
            wait(xb_r.at[o], r_xb.at[o])
            szb[o] = up_sum(o, (o - 1,), full).astype(BF16)
            send(szb.at[o], rzb.at[slot], s_zb, r_zb.at[slot], device)
        else:
            xs[...] = gate_sum(o, 1 - xh, (6, 7)).astype(BF16)
            send(xs, xr, s_h, r_h, across)
            ch[o % 2, xh, :, :HALF] = gate_sum(o, xh, (6, 7))
            wait(xb_r.at[o], r_xb.at[o])
            ch[o % 2, xh, :, HALF:] = up_sum(o, (6, 7), full)

    stage_all(0)
    stage_x(1)
    stage_x(2)
    stage_y(1)
    stage_x(3)
    wait(wg, s_w.at[0])
    wait(wu, s_w.at[1])
    own_row.wait()
    wait(listed_v.at[pl.ds(0, DP - 1)], r_act)
    to_smem = pltpu.make_async_copy(listed_v, listed, l_act)
    to_smem.start()
    to_smem.wait()
    for o in range(NZ):
        if 0 < o and o + 2 < NZ:
            stage_y(o + 2)
        if 0 < o and o + 3 < NZ:
            stage_x(o + 3)
        if 0 < o < NZ - 1:
            stage_f(o + 1)
        chip_sum(o)
        if o == 0:
            stage_f(1)
            stage_y(2)
        if o > 1:
            ring(o - 1)
        join(o)
        if o == 0:
            ring(0)
    ring(NZ - 1)

    wait(xr, r_h)
    gate = ch[(NZ - 1) % 2, xh, :, :HALF] + xr[...].astype(F32)
    up = ch[(NZ - 1) % 2, xh, :, HALF:]
    g = out_grad[...].astype(F32) * live[...]
    relu = jnp.maximum(gate, 0.0)
    gr[d, :, : CAP * BLOCK] = (g * up * 2.0 * relu).astype(BF16)
    gr[d, :, CAP * BLOCK :] = (g * relu * relu).astype(BF16)

    def own(zq, k):
        return gr.at[zq * 4 + k * 2 + c]

    def pass_on(zq, k, direction, distance):
        tile = own(zq, k)
        send(tile, tile, s_gz, r_gz.at[direction, distance, k], up_z if direction == 0 else down_z)

    def to_sibling(e, zq, k):
        tile = own(zq, k)
        send(tile, tile, s_gc, r_gc.at[e, k], sibling)

    send(gr.at[d], gr.at[d], s_gh, r_gh, across)
    pass_on(z, xh, 0, 0)
    pass_on(z, xh, 1, 0)
    to_sibling(0, z, xh)
    wait(own(z, 1 - xh), r_gh)
    pass_on(z, 1 - xh, 0, 0)
    pass_on(z, 1 - xh, 1, 0)
    to_sibling(0, z, 1 - xh)

    arrivals = [plane(k) for k in (0, -1, 1, -2, 2, -3, 3, 4)]

    def arrive(distance):
        for k in (0, 1):
            for direction in (0, 1):
                e = 1 + 2 * distance + direction
                zq = arrivals[e]
                wait(own(zq, k), r_gz.at[direction, distance, k])
                if distance < 2 or k == direction:
                    pass_on(zq, k, direction, distance + 1)
                to_sibling(e, zq, k)

    def arrive_last():
        for k in (0, 1):
            wait(own(arrivals[7], k), r_gz.at[k, 3, k])
            to_sibling(7, arrivals[7], k)

    def backward(e):
        zq = arrivals[e]
        for k in (0, 1):
            wait(gr.at[zq * 4 + k * 2 + 1 - c], r_gc.at[e, k])

        def one(k, _):
            q = zq * 4 + k
            grads = gr[q]
            value = lax.dot_general(grads, tile_weights(q), (((1,), (1,)), ((), ())), preferred_element_type=F32)
            part[:, :, q] = value.astype(BF16).reshape(2, 4, SHARE, ROWS)
            value = lax.dot_general(tile_tokens(q), grads, (((0,), (0,)), ((), ())), preferred_element_type=F32)
            piece[q] = value.astype(BF16)
            return 0

        lax.fori_loop(0, 4, one, 0)
        pltpu.make_async_copy(piece.at[four(zq)], pieces_hbm.at[four(zq)], s_p).start()
        first, second = pl.ds(zq * 4, 2), pl.ds(zq * 4 + 2, 2)
        send(part.at[:, y_far, first], yr1.at[0, e], s_0, r_0.at[0, e], up_y)
        send(part.at[:, y_far, second], yr1.at[1, e], s_0, r_0.at[1, e], down_y)

    def reduce_1(e):
        zq = arrivals[e]
        for direction, y_to, device in ((0, y_next, up_y), (1, y_last, down_y)):
            wait(yr1.at[direction, e], r_0.at[direction, e])
            half = pl.ds(zq * 4 + 2 * direction, 2)
            part[:, y_to, half] = (part[:, y_to, half].astype(F32) + yr1[direction, e].astype(F32)).astype(BF16)
            send(part.at[:, y_to, four(zq)], yr2.at[direction, e], s_1, r_1.at[direction, e], device)

    def reduce_2(e):
        zq = arrivals[e]
        for direction in (0, 1):
            wait(yr2.at[direction, e], r_1.at[direction, e])
        total = part[:, y, four(zq)].astype(F32) + yr2[0, e].astype(F32) + yr2[1, e].astype(F32)
        part[:, y, four(zq)] = total.astype(BF16)
        send(part.at[1 - xl, y, four(zq)], xr2.at[e], s_2, r_2.at[e], beside)

    def reduce_3(e):
        zq = arrivals[e]
        wait(xr2.at[e], r_2.at[e])
        fin[four(zq)] = (part[xl, y, four(zq)].astype(F32) + xr2[e].astype(F32)).astype(BF16)

        def home(k, _):
            q = zq * 4 + k
            dst = back.at[z, :, quarter_columns(a)]

            @pl.when(q != d)
            def _():
                send(fin.at[q], dst, s_o, r_o.at[z], (q, t))

            @pl.when(q == d)
            def _():
                pltpu.make_async_copy(fin.at[q], dst, r_o.at[z]).start()

            return 0

        lax.fori_loop(0, 4, home, 0)

    def to_owner(e):
        far = plane((0, 1, -1, 2, -2, 3, -3, 4)[e])
        wait(back.at[far], r_o.at[far])
        dst = out.at[share_rows(t)]

        @pl.when(far != t)
        def _():
            send(back.at[far], dst, s_out, r_out, (d, far))

        @pl.when(far == t)
        def _():
            pltpu.make_async_copy(back.at[far], dst, r_out).start()

    backward(0)
    reduce_1(0)
    arrive(0)
    backward(1), backward(2)
    reduce_2(0)
    reduce_1(1), reduce_1(2)
    arrive(1)
    backward(3), backward(4)
    reduce_3(0), reduce_2(1), reduce_2(2)
    reduce_1(3), reduce_1(4)
    arrive(2)
    backward(5), backward(6)
    reduce_3(1), reduce_3(2), reduce_2(3), reduce_2(4), to_owner(0)
    reduce_1(5)
    arrive_last()
    backward(7)
    reduce_1(6)
    reduce_3(3), reduce_3(4), reduce_2(5)
    reduce_1(7)
    reduce_2(6), to_owner(1), to_owner(2)
    reduce_2(7)
    reduce_3(5), reduce_3(6), reduce_3(7)
    for e in range(3, NZ):
        to_owner(e)

    wait(out, r_out)

    wait(fin.at[pl.ds(0, DP - 1)], s_t1)
    wait(fin.at[pl.ds(0, DP - 1)], s_o)
    wait(ts.at[pl.ds(0, TENSOR - 1)], s_ts)
    wait(ts.at[pl.ds(0, TENSOR - 1)], s_out)
    wait(listed_v.at[pl.ds(0, DP - 1)], s_act)
    most = pl.ds(0, 4 * (NZ - 1))
    wait(fin.at[most], s_x0)
    wait(fin.at[most], s_x)
    wait(tok.at[0, :, most], s_y)
    wait(tok.at[0, pl.ds(0, 2), most], s_f)
    wait(sc, s_c)
    wait(sza, s_za)
    wait(szb, s_zb)
    wait(xb_s, s_xb)
    wait(xs, s_h)
    wait(gr.at[d], s_gh)
    wait(gr.at[pl.ds(0, 14)], s_gz)
    wait(gr.at[pl.ds(0, 16)], s_gc)
    wait(yr1, s_0)
    wait(yr2, s_1)
    wait(xr2, s_2)
    wait(piece, s_p)


def sum_kernel(listed, piece_ref, dgate_ref, dup_ref, count, slots):
    blocks = dgate_ref.shape[1] // BLOCK
    chunk = piece_ref.shape[1]

    @pl.when(pl.program_id(0) == 0)
    def _():
        def clear(b, _):
            count[b] = 0
            return 0

        lax.fori_loop(0, blocks, clear, 0)

        def enter(s, _):
            block = listed[s // CAP, 0, lax.rem(s, CAP)]
            at = count[block]
            slots[block * (DP * CAP) + at] = s
            count[block] = at + 1
            return 0

        lax.fori_loop(0, DP * CAP, enter, 0)

    def one_block(b, _):
        def add(i, sums):
            s = slots[b * (DP * CAP) + i]
            q, c = s // CAP, lax.rem(s, CAP)
            new = []
            for k, total in enumerate(sums):
                at = pl.ds(pl.multiple_of((k * CAP + c) * BLOCK, BLOCK), BLOCK)
                new.append(total + piece_ref[q, :, at].astype(F32))
            return tuple(new)

        nothing = jnp.zeros((chunk, BLOCK), F32)
        sums = lax.fori_loop(0, count[b], add, (nothing, nothing))
        at = pl.ds(pl.multiple_of(b * BLOCK, BLOCK), BLOCK)
        dgate_ref[:, at] = sums[0].astype(BF16)
        dup_ref[:, at] = sums[1].astype(BF16)
        return 0

    lax.fori_loop(0, blocks, one_block, 0)


def per_device(tokens, out_grad, active, w_gate, w_up):
    width = w_gate.shape[1]
    blocks = width // BLOCK
    act = jnp.pad(jnp.minimum(active.reshape(1, CAP), blocks - 1), ((0, 0), (0, BLOCK - CAP)))
    live = jnp.repeat(active.reshape(1, CAP) < blocks, BLOCK, axis=1).astype(F32)
    vmem = pl.BlockSpec(memory_space=pltpu.VMEM)
    anywhere = pl.BlockSpec(memory_space=pl.ANY)
    dma, v = pltpu.SemaphoreType.DMA, pltpu.VMEM
    tile = (TILE, UNITS)
    slab = (SHARE, ROWS)
    input_grad, pieces, listed = pl.pallas_call(
        main_kernel,
        in_specs=[vmem, vmem, vmem, vmem, anywhere, anywhere],
        out_specs=[vmem, anywhere, pl.BlockSpec(memory_space=pltpu.SMEM)],
        out_shape=[
            jax.ShapeDtypeStruct((TILE, QUARTERS * ROWS), BF16),
            jax.ShapeDtypeStruct((DP, ROWS, UNITS), BF16),
            jax.ShapeDtypeStruct((DP, 1, BLOCK), jnp.int32),
        ],
        scratch_shapes=[
            v((blocks, ROWS, BLOCK), BF16),
            v((blocks, ROWS, BLOCK), BF16),
            v((DP, 1, BLOCK), jnp.int32),
            v((2, 4, DP, *slab), BF16),
            v((NZ, 2, *tile), BF16),
            v((NZ, 2, *tile), BF16),
            v((NZ - 1, 2, TILE, HALF), BF16),
            v((NZ, 2, TILE, HALF), BF16),
            v((NZ - 1, TILE, HALF), BF16),
            v((NZ, TILE, HALF), BF16),
            v((NZ, TILE, HALF), BF16),
            v((NZ, TILE, HALF), BF16),
            v((2, 2, *tile), F32),
            v((TILE, HALF), BF16),
            v((TILE, HALF), BF16),
            v((DP, *tile), BF16),
            v((2, 4, DP, *slab), BF16),
            v((DP, ROWS, UNITS), BF16),
            v((2, NZ, 2, 2, *slab), BF16),
            v((2, NZ, 2, 4, *slab), BF16),
            v((NZ, 4, *slab), BF16),
            v((DP, *slab), BF16),
            v((TENSOR, SHARE, QUARTERS * ROWS), BF16),
            v((TENSOR, SHARE, QUARTERS * ROWS), BF16),
            dma, dma((NZ,)), dma, dma, dma, dma((2,)),
            dma, dma((NZ,)), dma, dma((2, NZ)), dma, dma((2, NZ)),
            dma, dma((NZ, 2)), dma, dma((NZ, 2)), dma, dma((NZ,)), dma, dma((NZ,)), dma, dma,
            dma, dma, dma, dma((2, 4, 2)), dma, dma((NZ, 2)),
            dma, dma((2, NZ)), dma, dma((2, NZ)), dma, dma((NZ,)),
            dma, dma((NZ,)), dma,
            dma, dma((NZ,)), dma, dma,
            dma, dma,
        ],
        compiler_params=pltpu.CompilerParams(
            collective_id=0, has_side_effects=True, vmem_limit_bytes=62 * 2**20
        ),
    )(tokens, out_grad.reshape(TILE, CAP * BLOCK), live, act, w_gate, w_up)

    chunk = 128
    some_rows = pl.BlockSpec((chunk, width), lambda r, *_: (r, 0))
    dgate, dup = pl.pallas_call(
        sum_kernel,
        grid_spec=pltpu.PrefetchScalarGridSpec(
            num_scalar_prefetch=1,
            grid=(ROWS // chunk,),
            in_specs=[pl.BlockSpec((DP, chunk, UNITS), lambda r, *_: (0, r, 0))],
            out_specs=[some_rows, some_rows],
            scratch_shapes=[pltpu.SMEM((blocks,), jnp.int32), pltpu.SMEM((blocks * DP * CAP,), jnp.int32)],
        ),
        out_shape=[jax.ShapeDtypeStruct((ROWS, width), BF16)] * 2,
        compiler_params=pltpu.CompilerParams(vmem_limit_bytes=60 * 2**20),
    )(listed, pieces)
    return input_grad, dgate, dup


def solution(mesh):
    placed = (
        P("dp", "tensor"),
        P("dp", "tensor", None),
        P("dp", "tensor", None),
        P("dp", "tensor"),
        P("dp", "tensor"),
    )
    return jax.shard_map(
        per_device,
        mesh=mesh,
        in_specs=placed,
        out_specs=(P("dp", "tensor"), P("dp", "tensor"), P("dp", "tensor")),
        check_vma=False,
    )
```

```python
import jax
import jax.numpy as jnp
from jax import lax
from jax.experimental import pallas as pl
from jax.experimental.pallas import tpu as pltpu
from jax.sharding import PartitionSpec as P

MESH = pl.DeviceIdType.MESH
BLOCK, TILE, CAP = 128, 256, 2
NZ, QUARTERS, TENSOR, DP = 8, 4, 8, 32
ROWS = 256
SHARE = TILE // TENSOR
UNITS = 2 * CAP * BLOCK
HALF = UNITS // 2
BF16, F32 = jnp.bfloat16, jnp.float32


def send(src, dst, send_sem, recv_sem, device):
    pltpu.make_async_remote_copy(
        src_ref=src, dst_ref=dst, send_sem=send_sem, recv_sem=recv_sem, device_id=device, device_id_type=MESH
    ).start()


def wait(ref, sem):
    pltpu.make_async_copy(ref, ref, sem).wait()


def main_kernel(
    tokens, out_grad, live, act, wg_hbm, wu_hbm,
    out, pieces_hbm, listed,
    wg, wu, listed_v, tok, sc, rc, sza, rza, szb, rzb, xb_s, xb_r, ch, xs, xr, gr, part, piece, yr1, yr2, xr2, fin, ts, back,
    s_t1, r_t1, s_act, r_act, l_act, s_w, s_x, r_x, s_y, r_y, s_f, r_f, s_c, r_c, s_za, r_za, s_zb, r_zb, s_xb, r_xb, s_h, r_h,
    s_gh, r_gh, s_gz, r_gz, s_gc, r_gc, s_0, r_0, s_1, r_1, s_2, r_2, s_o, r_o, s_p, s_ts, r_ts, s_out, r_out, s_x0, r_x0,
):
    d, t = lax.axis_index("dp"), lax.axis_index("tensor")
    z, a = d // QUARTERS, lax.rem(d, QUARTERS)
    xh, c = a // 2, lax.rem(a, 2)
    xl, y = t // 4, lax.rem(t, 4)

    def plane(dz):
        return lax.rem(z + dz + NZ, NZ)

    up_z, down_z = (plane(1) * 4 + a, t), (plane(-1) * 4 + a, t)
    sibling = (d + 1 - 2 * c, t)
    across = (z * 4 + (1 - xh) * 2 + c, t)
    beside = (d, (1 - xl) * 4 + y)
    y_next, y_last, y_far = lax.rem(y + 1, 4), lax.rem(y + 3, 4), lax.rem(y + 2, 4)
    up_y, down_y = (d, xl * 4 + y_next), (d, xl * 4 + y_last)

    barrier = pltpu.get_barrier_semaphore()

    def greet(device):
        pl.semaphore_signal(barrier, inc=1, device_id=device, device_id_type=MESH)

    def greet_dp(k, _):
        greet((lax.rem(d + k, DP), t))
        return 0

    def greet_plane(k, _):
        greet((d, lax.rem(t + k, TENSOR)))
        return 0

    lax.fori_loop(1, TENSOR, greet_plane, 0)
    lax.fori_loop(1, DP, greet_dp, 0)
    pl.semaphore_wait(barrier, TENSOR - 1 + DP - 1)

    def share_rows(s):
        return pl.ds(pl.multiple_of(s * SHARE, SHARE), SHARE)

    def to_plane(k, _):
        s = lax.rem(t + k, TENSOR)
        send(tokens.at[share_rows(s)], ts.at[t], s_ts, r_ts.at[t], (d, s))
        return 0

    pltpu.make_async_copy(tokens.at[share_rows(t)], ts.at[t], r_ts.at[t]).start()
    lax.fori_loop(1, TENSOR, to_plane, 0)

    def quarter_columns(k):
        return pl.ds(pl.multiple_of(k * ROWS, ROWS), ROWS)

    def to_rows(far):
        wait(ts.at[far], r_ts.at[far])

        def one(k, _):
            other = far * QUARTERS + k

            @pl.when(other != d)
            def _():
                send(ts.at[far, :, quarter_columns(k)], tok.at[xl, y, d], s_t1, r_t1.at[z], (other, t))

            @pl.when(other == d)
            def _():
                pltpu.make_async_copy(ts.at[far, :, quarter_columns(k)], tok.at[xl, y, d], r_t1.at[z]).start()

            return 0

        lax.fori_loop(0, QUARTERS, one, 0)

    for k in (4, -3, 3, -2, 2, -1, 1, 0):
        to_rows(plane(k))

    own_row = pltpu.make_async_copy(act, listed_v.at[d], l_act)
    own_row.start()

    def tell(k, _):
        send(act, listed_v.at[d], s_act, r_act, (lax.rem(d + k, DP), t))
        return 0

    lax.fori_loop(1, DP, tell, 0)

    def load_block(b, _):
        columns = pl.ds(pl.multiple_of(b * BLOCK, BLOCK), BLOCK)
        pltpu.make_async_copy(wg_hbm.at[:, columns], wg.at[b], s_w.at[0]).start()
        pltpu.make_async_copy(wu_hbm.at[:, columns], wu.at[b], s_w.at[1]).start()
        return 0

    lax.fori_loop(0, wg.shape[0], load_block, 0)

    order = [plane(k) for k in (4, 3, -3, 2, -2, 1, -1, 0)]

    def four(zq):
        return pl.ds(zq * 4, 4)

    def stage_all(o):
        mine = tok.at[xl, y, four(order[o])]
        wait(mine, r_t1.at[order[o]])

        def one(k, _):
            send(mine, mine, s_x0, r_x0, (d, lax.rem(t + k, TENSOR)))
            return 0

        lax.fori_loop(1, TENSOR, one, 0)

    def stage_x(o):
        mine = tok.at[xl, y, four(order[o])]
        wait(mine, r_t1.at[order[o]])
        send(mine, mine, s_x, r_x.at[o], beside)

    def stage_y(o):
        wait(tok.at[1 - xl, y, four(order[o])], r_x.at[o])
        both = tok.at[:, y, four(order[o])]
        send(both, both, s_y, r_y.at[0, o], up_y)
        send(both, both, s_y, r_y.at[1, o], down_y)

    def stage_f(o):
        first, second = pl.ds(order[o] * 4, 2), pl.ds(order[o] * 4 + 2, 2)
        wait(tok.at[:, y_last, four(order[o])], r_y.at[0, o])
        send(tok.at[:, y_last, first], tok.at[:, y_last, first], s_f, r_f.at[0, o], up_y)
        wait(tok.at[:, y_next, four(order[o])], r_y.at[1, o])
        send(tok.at[:, y_next, second], tok.at[:, y_next, second], s_f, r_f.at[1, o], down_y)

    def tile_weights(q):
        picked = [listed[q, 0, k] for k in range(CAP)]
        return jnp.concatenate([ref[b] for ref in (wg, wu) for b in picked], axis=1)

    def tile_tokens(q):
        return tok[:, :, q].reshape(TILE, ROWS)

    def partial_sum(q):
        return jnp.dot(tile_tokens(q), tile_weights(q), preferred_element_type=F32)

    def along(o):
        return up_z if o % 2 else down_z

    def chip_sum(o):
        if o == 0:
            wait(fin.at[pl.ds(0, 4 * (TENSOR - 1))], r_x0)
        else:
            wait(tok.at[:, y_far, pl.ds(order[o] * 4, 2)], r_f.at[0, o])
            wait(tok.at[:, y_far, pl.ds(order[o] * 4 + 2, 2)], r_f.at[1, o])

        def for_sibling(k, _):
            sc[o, k] = partial_sum(order[o] * 4 + k * 2 + 1 - c).astype(BF16)
            send(sc.at[o, k], rc.at[o, k], s_c, r_c.at[o, k], sibling)
            return 0

        lax.fori_loop(0, 2, for_sibling, 0)

        def for_me(k, _):
            ch[o % 2, k] = partial_sum(order[o] * 4 + k * 2 + c)
            return 0

        lax.fori_loop(0, 2, for_me, 0)

    def join(o):
        for k in (1 - xh, xh):
            wait(rc.at[o, k], r_c.at[o, k])
            ch[o % 2, k] += rc[o, k].astype(F32)
            if k is not xh:
                xb_s[o] = ch[o % 2, k, :, HALF:].astype(BF16)
                send(xb_s.at[o], xb_r.at[o], s_xb, r_xb.at[o], across)

    def gate_sum(o, k, slots):
        total = ch[o % 2, k, :, :HALF]
        for slot in slots:
            wait(rza.at[slot, k], r_za.at[slot, k])
            total = total + rza[slot, k].astype(F32)
        return total

    def up_sum(o, slots, rows):
        total = ch[o % 2, xh, rows, HALF:] + xb_r[o, rows].astype(F32)
        for slot in slots:
            wait(rzb.at[slot, rows], r_zb.at[slot])
            total = total + rzb[slot, rows].astype(F32)
        return total

    top, bottom, full = pl.ds(0, TILE // 2), pl.ds(TILE // 2, TILE // 2), pl.ds(0, TILE)

    def ring(o):
        if o == 0:
            for k, device in ((0, up_z), (1, down_z)):
                sza[o, k] = gate_sum(o, k, ()).astype(BF16)
                send(sza.at[o, k], rza.at[k, k], s_za, r_za.at[k, k], device)
            wait(xb_r.at[o], r_xb.at[o])
            for k, device, rows in ((0, up_z, top), (1, down_z, bottom)):
                szb[o, rows] = up_sum(o, (), rows).astype(BF16)
                send(szb.at[o, rows], rzb.at[k, rows], s_zb, r_zb.at[k], device)
            return
        device, slot = along(o), o + 1
        if o <= 2:
            for k in (o - 1, 2 - o):
                sza[o, k] = gate_sum(o, k, (o - 1,) if k == o - 1 else ()).astype(BF16)
                send(sza.at[o, k], rza.at[slot, k], s_za, r_za.at[slot, k], device)
            wait(xb_r.at[o], r_xb.at[o])
            for k, rows in ((0, top), (1, bottom)):
                szb[o, rows] = up_sum(o, (o - 1,) if k == o - 1 else (), rows).astype(BF16)
            send(szb.at[o], rzb.at[slot], s_zb, r_zb.at[slot], device)
        elif o <= 6:

            def one(k, _):
                sza[o, k] = gate_sum(o, k, (o - 1,)).astype(BF16)
                send(sza.at[o, k], rza.at[slot, k], s_za, r_za.at[slot, k], device)
                return 0

            lax.fori_loop(0, 2, one, 0)
            wait(xb_r.at[o], r_xb.at[o])
            szb[o] = up_sum(o, (o - 1,), full).astype(BF16)
            send(szb.at[o], rzb.at[slot], s_zb, r_zb.at[slot], device)
        else:
            xs[...] = gate_sum(o, 1 - xh, (6, 7)).astype(BF16)
            send(xs, xr, s_h, r_h, across)
            ch[o % 2, xh, :, :HALF] = gate_sum(o, xh, (6, 7))
            wait(xb_r.at[o], r_xb.at[o])
            ch[o % 2, xh, :, HALF:] = up_sum(o, (6, 7), full)

    stage_all(0)
    stage_x(1)
    stage_x(2)
    stage_y(1)
    stage_x(3)
    wait(wg, s_w.at[0])
    wait(wu, s_w.at[1])
    own_row.wait()
    wait(listed_v.at[pl.ds(0, DP - 1)], r_act)
    to_smem = pltpu.make_async_copy(listed_v, listed, l_act)
    to_smem.start()
    to_smem.wait()
    for o in range(NZ):
        if 0 < o and o + 2 < NZ:
            stage_y(o + 2)
        if 0 < o and o + 3 < NZ:
            stage_x(o + 3)
        if 0 < o < NZ - 1:
            stage_f(o + 1)
        chip_sum(o)
        if o == 0:
            stage_f(1)
            stage_y(2)
        if o > 1:
            ring(o - 1)
        join(o)
        if o == 0:
            ring(0)
    ring(NZ - 1)

    wait(xr, r_h)
    gate = ch[(NZ - 1) % 2, xh, :, :HALF] + xr[...].astype(F32)
    up = ch[(NZ - 1) % 2, xh, :, HALF:]
    g = out_grad[...].astype(F32) * live[...]
    relu = jnp.maximum(gate, 0.0)
    gr[d, :, : CAP * BLOCK] = (g * up * 2.0 * relu).astype(BF16)
    gr[d, :, CAP * BLOCK :] = (g * relu * relu).astype(BF16)

    def own(zq, k):
        return gr.at[zq * 4 + k * 2 + c]

    def pass_on(zq, k, direction, distance):
        tile = own(zq, k)
        send(tile, tile, s_gz, r_gz.at[direction, distance, k], up_z if direction == 0 else down_z)

    def to_sibling(e, zq, k):
        tile = own(zq, k)
        send(tile, tile, s_gc, r_gc.at[e, k], sibling)

    send(gr.at[d], gr.at[d], s_gh, r_gh, across)
    pass_on(z, xh, 0, 0)
    pass_on(z, xh, 1, 0)
    to_sibling(0, z, xh)
    wait(own(z, 1 - xh), r_gh)
    pass_on(z, 1 - xh, 0, 0)
    pass_on(z, 1 - xh, 1, 0)
    to_sibling(0, z, 1 - xh)

    arrivals = [plane(k) for k in (0, -1, 1, -2, 2, -3, 3, 4)]

    def arrive(distance):
        for k in (0, 1):
            for direction in (0, 1):
                e = 1 + 2 * distance + direction
                zq = arrivals[e]
                wait(own(zq, k), r_gz.at[direction, distance, k])
                if distance < 2 or k == direction:
                    pass_on(zq, k, direction, distance + 1)
                to_sibling(e, zq, k)

    def arrive_last():
        for k in (0, 1):
            wait(own(arrivals[7], k), r_gz.at[k, 3, k])
            to_sibling(7, arrivals[7], k)

    late = 5

    def piece_of(q, grads):
        value = lax.dot_general(tile_tokens(q), grads, (((0,), (0,)), ((), ())), preferred_element_type=F32)
        piece[q] = value.astype(BF16)

    def pieces(e):
        zq = arrivals[e]

        def one(k, _):
            piece_of(zq * 4 + k, gr[zq * 4 + k])
            return 0

        lax.fori_loop(0, 4, one, 0)
        pltpu.make_async_copy(piece.at[four(zq)], pieces_hbm.at[four(zq)], s_p).start()

    def backward(e):
        zq = arrivals[e]
        for k in (0, 1):
            wait(gr.at[zq * 4 + k * 2 + 1 - c], r_gc.at[e, k])

        def one(k, _):
            q = zq * 4 + k
            grads = gr[q]
            value = lax.dot_general(grads, tile_weights(q), (((1,), (1,)), ((), ())), preferred_element_type=F32)
            part[:, :, q] = value.astype(BF16).reshape(2, 4, SHARE, ROWS)
            if e < late:
                piece_of(q, grads)
            return 0

        lax.fori_loop(0, 4, one, 0)
        if e < late:
            pltpu.make_async_copy(piece.at[four(zq)], pieces_hbm.at[four(zq)], s_p).start()
        first, second = pl.ds(zq * 4, 2), pl.ds(zq * 4 + 2, 2)
        send(part.at[:, y_far, first], yr1.at[0, e], s_0, r_0.at[0, e], up_y)
        send(part.at[:, y_far, second], yr1.at[1, e], s_0, r_0.at[1, e], down_y)

    def reduce_1(e):
        zq = arrivals[e]
        for direction, y_to, device in ((0, y_next, up_y), (1, y_last, down_y)):
            wait(yr1.at[direction, e], r_0.at[direction, e])
            half = pl.ds(zq * 4 + 2 * direction, 2)
            part[:, y_to, half] = (part[:, y_to, half].astype(F32) + yr1[direction, e].astype(F32)).astype(BF16)
            send(part.at[:, y_to, four(zq)], yr2.at[direction, e], s_1, r_1.at[direction, e], device)

    def reduce_2(e):
        zq = arrivals[e]
        for direction in (0, 1):
            wait(yr2.at[direction, e], r_1.at[direction, e])
        total = part[:, y, four(zq)].astype(F32) + yr2[0, e].astype(F32) + yr2[1, e].astype(F32)
        part[:, y, four(zq)] = total.astype(BF16)
        send(part.at[1 - xl, y, four(zq)], xr2.at[e], s_2, r_2.at[e], beside)

    def reduce_3(e):
        zq = arrivals[e]
        wait(xr2.at[e], r_2.at[e])
        fin[four(zq)] = (part[xl, y, four(zq)].astype(F32) + xr2[e].astype(F32)).astype(BF16)

        def home(k, _):
            q = zq * 4 + k
            dst = back.at[z, :, quarter_columns(a)]

            @pl.when(q != d)
            def _():
                send(fin.at[q], dst, s_o, r_o.at[z], (q, t))

            @pl.when(q == d)
            def _():
                pltpu.make_async_copy(fin.at[q], dst, r_o.at[z]).start()

            return 0

        lax.fori_loop(0, 4, home, 0)

    def to_owner(e):
        far = plane((0, 1, -1, 2, -2, 3, -3, 4)[e])
        wait(back.at[far], r_o.at[far])
        dst = out.at[share_rows(t)]

        @pl.when(far != t)
        def _():
            send(back.at[far], dst, s_out, r_out, (d, far))

        @pl.when(far == t)
        def _():
            pltpu.make_async_copy(back.at[far], dst, r_out).start()

    backward(0)
    reduce_1(0)
    arrive(0)
    backward(1), backward(2)
    reduce_2(0)
    reduce_1(1), reduce_1(2)
    arrive(1)
    backward(3), backward(4)
    reduce_3(0), reduce_2(1), reduce_2(2)
    reduce_1(3), reduce_1(4)
    arrive(2)
    backward(5), backward(6)
    reduce_3(1), reduce_3(2), reduce_2(3), reduce_2(4), to_owner(0)
    reduce_1(5)
    arrive_last()
    backward(7)
    reduce_1(6)
    reduce_3(3), reduce_3(4), reduce_2(5)
    reduce_1(7)
    pieces(5)
    reduce_2(6), to_owner(1), to_owner(2)
    pieces(6)
    reduce_2(7)
    reduce_3(5), reduce_3(6)
    pieces(7)
    reduce_3(7)
    for e in range(3, NZ):
        to_owner(e)

    wait(out, r_out)

    wait(fin.at[pl.ds(0, DP - 1)], s_t1)
    wait(fin.at[pl.ds(0, DP - 1)], s_o)
    wait(ts.at[pl.ds(0, TENSOR - 1)], s_ts)
    wait(ts.at[pl.ds(0, TENSOR - 1)], s_out)
    wait(listed_v.at[pl.ds(0, DP - 1)], s_act)
    most = pl.ds(0, 4 * (NZ - 1))
    wait(fin.at[most], s_x0)
    wait(fin.at[most], s_x)
    wait(tok.at[0, :, most], s_y)
    wait(tok.at[0, pl.ds(0, 2), most], s_f)
    wait(sc, s_c)
    wait(sza, s_za)
    wait(szb, s_zb)
    wait(xb_s, s_xb)
    wait(xs, s_h)
    wait(gr.at[d], s_gh)
    wait(gr.at[pl.ds(0, 14)], s_gz)
    wait(gr.at[pl.ds(0, 16)], s_gc)
    wait(yr1, s_0)
    wait(yr2, s_1)
    wait(xr2, s_2)
    wait(piece, s_p)


def sum_kernel(listed, piece_ref, dgate_ref, dup_ref, count, slots):
    blocks = dgate_ref.shape[1] // BLOCK
    chunk = piece_ref.shape[1]

    @pl.when(pl.program_id(0) == 0)
    def _():
        def clear(b, _):
            count[b] = 0
            return 0

        lax.fori_loop(0, blocks, clear, 0)

        def enter(s, _):
            block = listed[s // CAP, 0, lax.rem(s, CAP)]
            at = count[block]
            slots[block * (DP * CAP) + at] = s
            count[block] = at + 1
            return 0

        lax.fori_loop(0, DP * CAP, enter, 0)

    def one_block(b, _):
        def add(i, sums):
            s = slots[b * (DP * CAP) + i]
            q, c = s // CAP, lax.rem(s, CAP)
            new = []
            for k, total in enumerate(sums):
                at = pl.ds(pl.multiple_of((k * CAP + c) * BLOCK, BLOCK), BLOCK)
                new.append(total + piece_ref[q, :, at].astype(F32))
            return tuple(new)

        nothing = jnp.zeros((chunk, BLOCK), F32)
        sums = lax.fori_loop(0, count[b], add, (nothing, nothing))
        at = pl.ds(pl.multiple_of(b * BLOCK, BLOCK), BLOCK)
        dgate_ref[:, at] = sums[0].astype(BF16)
        dup_ref[:, at] = sums[1].astype(BF16)
        return 0

    lax.fori_loop(0, blocks, one_block, 0)


def per_device(tokens, out_grad, active, w_gate, w_up):
    width = w_gate.shape[1]
    blocks = width // BLOCK
    act = jnp.pad(jnp.minimum(active.reshape(1, CAP), blocks - 1), ((0, 0), (0, BLOCK - CAP)))
    live = jnp.repeat(active.reshape(1, CAP) < blocks, BLOCK, axis=1).astype(F32)
    vmem = pl.BlockSpec(memory_space=pltpu.VMEM)
    anywhere = pl.BlockSpec(memory_space=pl.ANY)
    dma, v = pltpu.SemaphoreType.DMA, pltpu.VMEM
    tile = (TILE, UNITS)
    slab = (SHARE, ROWS)
    input_grad, pieces, listed = pl.pallas_call(
        main_kernel,
        in_specs=[vmem, vmem, vmem, vmem, anywhere, anywhere],
        out_specs=[vmem, anywhere, pl.BlockSpec(memory_space=pltpu.SMEM)],
        out_shape=[
            jax.ShapeDtypeStruct((TILE, QUARTERS * ROWS), BF16),
            jax.ShapeDtypeStruct((DP, ROWS, UNITS), BF16),
            jax.ShapeDtypeStruct((DP, 1, BLOCK), jnp.int32),
        ],
        scratch_shapes=[
            v((blocks, ROWS, BLOCK), BF16),
            v((blocks, ROWS, BLOCK), BF16),
            v((DP, 1, BLOCK), jnp.int32),
            v((2, 4, DP, *slab), BF16),
            v((NZ, 2, *tile), BF16),
            v((NZ, 2, *tile), BF16),
            v((NZ - 1, 2, TILE, HALF), BF16),
            v((NZ, 2, TILE, HALF), BF16),
            v((NZ - 1, TILE, HALF), BF16),
            v((NZ, TILE, HALF), BF16),
            v((NZ, TILE, HALF), BF16),
            v((NZ, TILE, HALF), BF16),
            v((2, 2, *tile), F32),
            v((TILE, HALF), BF16),
            v((TILE, HALF), BF16),
            v((DP, *tile), BF16),
            v((2, 4, DP, *slab), BF16),
            v((DP, ROWS, UNITS), BF16),
            v((2, NZ, 2, 2, *slab), BF16),
            v((2, NZ, 2, 4, *slab), BF16),
            v((NZ, 4, *slab), BF16),
            v((DP, *slab), BF16),
            v((TENSOR, SHARE, QUARTERS * ROWS), BF16),
            v((TENSOR, SHARE, QUARTERS * ROWS), BF16),
            dma, dma((NZ,)), dma, dma, dma, dma((2,)),
            dma, dma((NZ,)), dma, dma((2, NZ)), dma, dma((2, NZ)),
            dma, dma((NZ, 2)), dma, dma((NZ, 2)), dma, dma((NZ,)), dma, dma((NZ,)), dma, dma,
            dma, dma, dma, dma((2, 4, 2)), dma, dma((NZ, 2)),
            dma, dma((2, NZ)), dma, dma((2, NZ)), dma, dma((NZ,)),
            dma, dma((NZ,)), dma,
            dma, dma((NZ,)), dma, dma,
            dma, dma,
        ],
        compiler_params=pltpu.CompilerParams(
            collective_id=0, has_side_effects=True, vmem_limit_bytes=62 * 2**20
        ),
    )(tokens, out_grad.reshape(TILE, CAP * BLOCK), live, act, w_gate, w_up)

    chunk = 128
    some_rows = pl.BlockSpec((chunk, width), lambda r, *_: (r, 0))
    dgate, dup = pl.pallas_call(
        sum_kernel,
        grid_spec=pltpu.PrefetchScalarGridSpec(
            num_scalar_prefetch=1,
            grid=(ROWS // chunk,),
            in_specs=[pl.BlockSpec((DP, chunk, UNITS), lambda r, *_: (0, r, 0))],
            out_specs=[some_rows, some_rows],
            scratch_shapes=[pltpu.SMEM((blocks,), jnp.int32), pltpu.SMEM((blocks * DP * CAP,), jnp.int32)],
        ),
        out_shape=[jax.ShapeDtypeStruct((ROWS, width), BF16)] * 2,
        compiler_params=pltpu.CompilerParams(vmem_limit_bytes=60 * 2**20),
    )(listed, pieces)
    return input_grad, dgate, dup


def solution(mesh):
    placed = (
        P("dp", "tensor"),
        P("dp", "tensor", None),
        P("dp", "tensor", None),
        P("dp", "tensor"),
        P("dp", "tensor"),
    )
    return jax.shard_map(
        per_device,
        mesh=mesh,
        in_specs=placed,
        out_specs=(P("dp", "tensor"), P("dp", "tensor"), P("dp", "tensor")),
        check_vma=False,
    )
```
